32 devices in a mesh: aux: 4 (over x, core), basis: 8 (over z, y).
Axes of the slice: x: 2, y: 2, z: 4, core: 2. Of those that a mesh axis runs over, the one named last changes fastest.
Arguments:
- v_blocks: bfloat16 [32, 384, 128, 128], P('aux', 'basis'), may hold values from -6 to 6
- pair_map: int32 [4, 384, 2], P('aux', 'basis'), may hold values from 0 to 239, as said below
- pair_count: int32 [4, 8], P('aux', 'basis'), may hold values from 2 to 48, as said below
- occ_coef: bfloat16 [8, 30720], P(None, 'basis'), may hold values from -0.375 to 0.375
- virt_coef: bfloat16 [30720, 32768], P('basis', 'aux'), may hold values from -0.03125 to 0.03125
Outputs:
- b_tensor: bfloat16 [32768, 256], P(('aux', 'basis'))
The draws below stay inside these ranges and needn't reach their ends.
Inputs may be any that keep to these rules, and one draw needn't show every extreme that they name: pair_map[s, k, 0] lies in the blocks of basis index k // 48 (blocks b * 240 / 8 onward); pair_map[s, k, 1] lies within 8 blocks of it, cyclically over 240 blocks, and that distance 8 is reached. Only the first pair_count slots of a device are live; in every slab some basis index has all 48 live.
All inputs are finite; a program needn't handle non-finite values.
Results may differ from the reference program's by a relative error of at most 0.0049.
Values may be sent and summed in bfloat16 or wider, within the bound.
No kernel may reach another device: no remote copies, remote signals or barrier semaphores. Data moves between devices by JAX's collectives and lax.ppermute only.
A program may use at most 192 MiB of HBM per device.

```python
import jax
import jax.numpy as jnp
from jax import lax

NBF = 30720
BB = 128
NVIR = 32768
NOCC = 8
NEAR = 8
P_DEV = 8
PAIR_CAP = 48
NB = 240
NAUXW = 32
PAIRS = 384
N_AUX = 4
N_BASIS = 8


def draw_pair_count(key, part):
    key_centre, key_jitter = jax.random.split(jax.random.fold_in(key, 11))
    centre = jax.random.randint(key_centre, (N_AUX, 1), 0, N_BASIS)
    devices = jnp.arange(N_BASIS)[None, :]
    distance = jnp.abs(devices - centre)
    distance = jnp.minimum(distance, N_BASIS - distance)
    base_count = PAIR_CAP * 4 // (4 + distance)
    jitter = jax.random.randint(key_jitter, (N_AUX, N_BASIS), 0, 3)
    counts = jnp.where(distance == 0, PAIR_CAP, jnp.maximum(base_count - jitter, 2))
    return counts.astype(jnp.int32)


def draw_pair_map(key, part):
    key_mu, key_nu = jax.random.split(jax.random.fold_in(key, 23))
    blocks_here = NB // N_BASIS
    local_block = jax.random.randint(key_mu, (N_AUX, N_BASIS, PAIR_CAP), 0, blocks_here)
    mu_block = local_block + jnp.arange(N_BASIS)[None, :, None] * blocks_here
    offsets = jax.random.randint(key_nu, (N_AUX, N_BASIS, PAIR_CAP), -NEAR, NEAR + 1)
    slot_index = jnp.arange(PAIR_CAP)[None, None, :]
    offsets = jnp.where(slot_index == 0, NEAR, jnp.where(slot_index == 1, -NEAR, offsets))
    nu_block = jnp.mod(mu_block + offsets, NB)
    stacked = jnp.stack([mu_block, nu_block], axis=-1)
    return stacked.reshape(N_AUX, N_BASIS * PAIR_CAP, 2).astype(jnp.int32)


def block_scale(stream_key, shape, pieces, low, high):
    def one(position, shards_of):
        steps = jax.random.uniform(jax.random.fold_in(jax.random.fold_in(stream_key, 6), position), (shards_of,), jnp.float32, low / len(pieces), high / len(pieces))
        return jnp.repeat(jnp.exp(steps), shape[position] // shards_of).reshape((-1,) + (1,) * (len(shape) - position - 1))

    level = one(*pieces[0])
    for cut in pieces[1:]:
        level = level * one(*cut)
    return level


def centred(stream_key, shape, scale, reach, cuts=(), dtype=jnp.bfloat16):
    drawn = scale * jax.random.normal(stream_key, shape, jnp.float32)
    if cuts:
        drawn = drawn * block_scale(stream_key, shape, cuts, -0.22, 0.18)
    return jnp.clip(drawn, -reach, reach).astype(dtype)


def setup_inputs(seed: int = 0) -> dict:
    key_list = jax.random.split(jax.random.key(seed), 6)
    v_blocks = centred(key_list[0], (NAUXW, PAIRS, BB, BB), 1.0, 6.0, ((0, 4), (1, 8)))
    pair_map = draw_pair_map(jax.random.fold_in(key_list[5], 71), 0)
    pair_count = draw_pair_count(jax.random.fold_in(key_list[5], 71), 0)
    occ_coef = centred(key_list[3], (NOCC, NBF), (2 * BB) ** -0.5, 0.375, ((1, 8),))
    virt_coef = centred(key_list[4], (NBF, NVIR), NBF ** -0.5, 0.03125, ((0, 8), (1, 4)))
    return dict(v_blocks=v_blocks, pair_map=pair_map, pair_count=pair_count, occ_coef=occ_coef, virt_coef=virt_coef)


def reference(v_blocks, pair_map, pair_count, occ_coef, virt_coef):
    occ_table = occ_coef.astype(jnp.float32).reshape(NOCC, NB, BB)
    slot_index = jnp.arange(N_BASIS * PAIR_CAP).astype(jnp.int32)
    slab_list = []
    for slab in range(N_AUX):
        mu_block = pair_map[slab, :, 0]
        nu_block = pair_map[slab, :, 1]
        live_slots = ((slot_index % PAIR_CAP) < pair_count[slab, slot_index // PAIR_CAP]).astype(jnp.float32)
        picked = jnp.take(occ_table, nu_block, axis=1)
        slab_blocks = v_blocks[slab * P_DEV:(slab + 1) * P_DEV].astype(jnp.float32)
        half_sums = jnp.einsum("qkmn,ikn->qikm", slab_blocks, picked, precision=lax.Precision.HIGHEST)
        half_sums = half_sums * live_slots[None, None, :, None]
        owner_map = (mu_block[:, None] == jnp.arange(NB).astype(jnp.int32)[None, :]).astype(jnp.float32)
        local_half = jnp.einsum("qikm,kb->qibm", half_sums, owner_map, precision=lax.Precision.HIGHEST)
        slab_list.append(local_half.reshape(P_DEV * NOCC, NBF).astype(jnp.bfloat16))
    half_rows = jnp.concatenate(slab_list, axis=0)
    result = lax.dot_general(virt_coef, half_rows, (((0,), (1,)), ((), ())), preferred_element_type=jnp.float32)
    return result.astype(jnp.bfloat16)
```

```python
import functools

import jax
import jax.numpy as jnp
from jax import lax
from jax.experimental import pallas as pl
from jax.experimental.pallas import tpu as pltpu
from jax.sharding import PartitionSpec as P

BB = 128
NEAR = 8
F32 = jnp.float32
BF16 = jnp.bfloat16


def exchange(array, axis, bit):
    peers = lax.axis_size(axis)
    return lax.ppermute(array, axis, [(i, i ^ bit) for i in range(peers)])


def shift(array, axis, step):
    peers = lax.axis_size(axis)
    return lax.ppermute(array, axis, [(i, (i + step) % peers) for i in range(peers)])


def divisor(length, most):
    return max(d for d in range(1, most + 1) if length % d == 0)


def half_kernel(per, mu_ref, pos_ref, count_ref, own_ref, before_ref, after_ref, v_ref, out_ref, acc_ref, occ_ref):
    step = pl.program_id(0)
    q = v_ref.shape[0]
    nocc = own_ref.shape[0]
    halo = before_ref.shape[1]
    here = own_ref.shape[1]

    @pl.when(step == 0)
    def _():
        acc_ref[...] = jnp.zeros_like(acc_ref)
        occ_ref[:, :halo] = before_ref[...]
        occ_ref[:, halo : halo + here] = own_ref[...]
        occ_ref[:, halo + here :] = after_ref[...]

    for j in range(per):
        k = step * per + j
        source = pl.multiple_of(pos_ref[k] * BB, BB)
        picked = occ_ref[:, pl.ds(source, BB)]
        picked = jnp.where(k < count_ref[0], picked, jnp.zeros_like(picked))
        blocks = v_ref[:, j].reshape(q * BB, BB)
        rows = lax.dot_general(picked, blocks, (((1,), (1,)), ((), ())), preferred_element_type=F32)
        target = pl.multiple_of(mu_ref[k] * BB, BB)
        for p in range(q):
            acc_ref[p * nocc : (p + 1) * nocc, pl.ds(target, BB)] += rows[:, p * BB : (p + 1) * BB]

    @pl.when(step == pl.num_programs(0) - 1)
    def _():
        out_ref[...] = acc_ref[...].astype(BF16)


def half_rows(v_blocks, mu, position, count, own, before, after):
    q, pairs = v_blocks.shape[:2]
    nocc, here = own.shape
    halo = before.shape[1]
    per = divisor(pairs, 8)
    whole = lambda k, *_: (0, 0)
    return pl.pallas_call(
        functools.partial(half_kernel, per),
        grid_spec=pltpu.PrefetchScalarGridSpec(
            num_scalar_prefetch=3,
            grid=(pairs // per,),
            in_specs=[
                pl.BlockSpec((nocc, here), whole),
                pl.BlockSpec((nocc, halo), whole),
                pl.BlockSpec((nocc, halo), whole),
                pl.BlockSpec((q, per, BB, BB), lambda k, *_: (0, k, 0, 0)),
            ],
            out_specs=pl.BlockSpec((q * nocc, here), whole),
            scratch_shapes=[
                pltpu.VMEM((q * nocc, here), F32),
                pltpu.VMEM((nocc, here + 2 * halo), BF16),
            ],
        ),
        out_shape=jax.ShapeDtypeStruct((q * nocc, here), BF16),
        compiler_params=pltpu.CompilerParams(vmem_limit_bytes=24 * 2**20),
        cost_estimate=pl.CostEstimate(
            flops=2 * v_blocks.size * nocc, bytes_accessed=2 * v_blocks.size, transcendentals=0
        ),
    )(mu, position, count, own, before, after, v_blocks)


def chunk_kernel(chunk_ref, half_ref, virt_ref, *refs):
    *adds, out_ref = refs
    total = jnp.dot(half_ref[...], virt_ref[...], preferred_element_type=F32)
    for add in adds:
        total += add[...].astype(F32)
    out_ref[...] = total.astype(BF16)


def chunk_product(chunk, half, virt, width, adds=()):
    rows, depth = half.shape
    tile = divisor(width, 256)
    tiles = width // tile
    return pl.pallas_call(
        chunk_kernel,
        grid_spec=pltpu.PrefetchScalarGridSpec(
            num_scalar_prefetch=1,
            grid=(tiles,),
            in_specs=[
                pl.BlockSpec((rows, depth), lambda t, c: (0, 0)),
                pl.BlockSpec((depth, tile), lambda t, c: (0, c[0] * tiles + t)),
            ]
            + [pl.BlockSpec((rows, tile), lambda t, c: (0, t))] * len(adds),
            out_specs=pl.BlockSpec((rows, tile), lambda t, c: (0, t)),
        ),
        out_shape=jax.ShapeDtypeStruct((rows, width), BF16),
        compiler_params=pltpu.CompilerParams(vmem_limit_bytes=24 * 2**20),
        cost_estimate=pl.CostEstimate(
            flops=2 * rows * depth * width, bytes_accessed=2 * depth * (width + rows), transcendentals=0
        ),
    )(chunk.reshape(1), half, virt, *adds)


def last_kernel(slab, chunk_ref, aux_ref, half_ref, virt_ref, *refs):
    *adds, out_ref, total_ref = refs
    total = jnp.dot(half_ref[...], virt_ref[...], preferred_element_type=F32)
    for add in adds:
        total += add[...].astype(F32)
    total_ref[...] = total
    slabs = total.shape[0] // slab
    ordered = [
        total_ref[pl.ds(pl.multiple_of((aux_ref[0] ^ s) * slab, slab), slab), :] for s in range(slabs)
    ]
    out_ref[...] = jnp.concatenate(ordered, axis=0).T.astype(BF16)


def last_product(chunk, aux, half, virt, width, slab, adds):
    rows, depth = half.shape
    tile = divisor(width, 256)
    tiles = width // tile
    return pl.pallas_call(
        functools.partial(last_kernel, slab),
        grid_spec=pltpu.PrefetchScalarGridSpec(
            num_scalar_prefetch=2,
            grid=(tiles,),
            in_specs=[
                pl.BlockSpec((rows, depth), lambda t, c, x: (0, 0)),
                pl.BlockSpec((depth, tile), lambda t, c, x: (0, c[0] * tiles + t)),
            ]
            + [pl.BlockSpec((rows, tile), lambda t, c, x: (0, t))] * len(adds),
            out_specs=pl.BlockSpec((tile, rows), lambda t, c, x: (t, 0)),
            scratch_shapes=[pltpu.VMEM((rows, tile), F32)],
        ),
        out_shape=jax.ShapeDtypeStruct((width, rows), BF16),
        compiler_params=pltpu.CompilerParams(vmem_limit_bytes=24 * 2**20),
        cost_estimate=pl.CostEstimate(
            flops=2 * rows * depth * width, bytes_accessed=2 * depth * (width + rows), transcendentals=0
        ),
    )(chunk.reshape(1), aux.reshape(1), half, virt, *adds)


def local(v_blocks, pair_map, pair_count, occ_coef, virt_coef):
    peers = lax.axis_size("basis")
    slabs = lax.axis_size("aux")
    aux = lax.axis_index("aux")
    basis = lax.axis_index("basis")
    blocks_here = virt_coef.shape[0] // BB
    blocks = blocks_here * peers
    first_block = basis * blocks_here
    halo = NEAR * BB

    before = shift(occ_coef[:, -halo:], "basis", 1)
    after = shift(occ_coef[:, :halo], "basis", -1)
    mu = pair_map[0, :, 0] - first_block
    position = jnp.mod(pair_map[0, :, 1] - first_block + NEAR, blocks)
    own = half_rows(v_blocks, mu, position, pair_count.reshape(1), occ_coef, before, after)

    held = {0: own}
    bit = slabs // 2
    while bit >= 1:
        for r in sorted(held):
            held[r ^ bit] = exchange(held[r], "aux", bit)
        bit //= 2
    half = jnp.concatenate([held[r] for r in range(slabs)], axis=0)

    width = virt_coef.shape[1] // peers
    groups = peers // 2
    group, side = basis // 2, basis % 2
    steps = sorted(range(1, groups), key=lambda d: -min(d, groups - d)) + [0]
    chunk_of = lambda step, s: (2 * ((group + step) % groups) + s).astype(jnp.int32)
    received = {}
    for step in steps:
        sent = chunk_product(chunk_of(step, 1 - side), half, virt_coef, width)
        received[step] = exchange(sent, "basis", 1)
    arrived = []
    for step in steps[:-1]:
        sent = chunk_product(chunk_of(step, side), half, virt_coef, width, (received[step],))
        arrived.append(shift(sent, "basis", 2 * step))
    return last_product(
        chunk_of(0, side), aux, half, virt_coef, width, own.shape[0], (received[0], *arrived)
    )


def solution(mesh):
    in_specs = (
        P("aux", "basis", None, None),
        P("aux", "basis", None),
        P("aux", "basis"),
        P(None, "basis"),
        P("basis", "aux"),
    )
    out_specs = P(("aux", "basis"), None)
    return jax.shard_map(local, mesh=mesh, in_specs=in_specs, out_specs=out_specs, check_vma=False)
```

```python
import functools

import jax
import jax.numpy as jnp
from jax import lax
from jax.experimental import pallas as pl
from jax.experimental.pallas import tpu as pltpu
from jax.sharding import PartitionSpec as P

BB = 128
NEAR = 8
F32 = jnp.float32
BF16 = jnp.bfloat16
VMEM = pl.BlockSpec(memory_space=pltpu.VMEM)
SMEM = pl.BlockSpec(memory_space=pltpu.SMEM)
HBM = pl.BlockSpec(memory_space=pltpu.HBM)
ANY = pl.BlockSpec(memory_space=pl.ANY)


def exchange(array, axis, bit):
    peers = lax.axis_size(axis)
    return lax.ppermute(array, axis, [(i, i ^ bit) for i in range(peers)])


def divisor(length, most):
    return max(d for d in range(1, most + 1) if length % d == 0)


def half_kernel(groups, blocks, basis_ref, map_ref, count_ref, own_ref, pair_ref, next_ref, v_ref, out_ref, buf_ref, acc_ref, occ_ref, sems):
    q = v_ref.shape[0]
    nocc, here = own_ref.shape
    halo = pair_ref.shape[1]
    per = v_ref.shape[1] // groups
    blocks_here = here // BB
    first = basis_ref[0] * blocks_here
    copies = [
        pltpu.make_async_copy(v_ref.at[:, pl.ds(g * per, per)], buf_ref.at[g], sems.at[g]) for g in range(groups)
    ]
    for copy in copies:
        copy.start()

    acc_ref[...] = jnp.zeros_like(acc_ref)
    odd = basis_ref[0] % 2
    occ_ref[:, halo : halo + here] = own_ref[...]
    occ_ref[:, pl.ds(pl.multiple_of((1 - odd) * (halo + here), BB), halo)] = pair_ref[...]
    occ_ref[:, pl.ds(pl.multiple_of(odd * (halo + here), BB), halo)] = next_ref[...]

    def picked(k):
        source = lax.rem(map_ref[0, k, 1] - first + NEAR + blocks, blocks)
        rows = occ_ref[:, pl.ds(pl.multiple_of(source * BB, BB), BB)]
        return jnp.where(k < count_ref[0, 0], rows, jnp.zeros_like(rows))

    for g in range(groups):
        copies[g].wait()
        sums = []
        for j in range(0, per, 2):
            k = g * per + j
            if j + 1 < per:
                one, two = picked(k), picked(k + 1)
                none = jnp.zeros_like(one)
                left = jnp.concatenate(
                    [jnp.concatenate([one, none], axis=1), jnp.concatenate([none, two], axis=1)], axis=0
                )
                right = jnp.concatenate([buf_ref[g, :, j], buf_ref[g, :, j + 1]], axis=-1).reshape(q * BB, 2 * BB)
            else:
                left, right = picked(k), buf_ref[g, :, j].reshape(q * BB, BB)
            sums.append(lax.dot_general(left, right, (((1,), (1,)), ((), ())), preferred_element_type=F32))
        for j in range(per):
            rows = sums[j // 2][(j % 2) * nocc : (j % 2 + 1) * nocc]
            target = pl.multiple_of((map_ref[0, g * per + j, 0] - first) * BB, BB)
            for p in range(q):
                acc_ref[p * nocc : (p + 1) * nocc, pl.ds(target, BB)] += rows[:, p * BB : (p + 1) * BB]
    out_ref[...] = acc_ref[...].astype(BF16)


def half_rows(basis, pair_map, pair_count, own, pair, after, v_blocks, blocks):
    q, pairs = v_blocks.shape[:2]
    nocc, here = own.shape
    halo = pair.shape[1]
    groups = pairs // divisor(pairs, 8)
    return pl.pallas_call(
        functools.partial(half_kernel, groups, blocks),
        in_specs=[SMEM, SMEM, SMEM, VMEM, VMEM, VMEM, HBM],
        out_specs=VMEM,
        scratch_shapes=[
            pltpu.VMEM((groups, q, pairs // groups, BB, BB), BF16),
            pltpu.VMEM((q * nocc, here), F32),
            pltpu.VMEM((nocc, here + 2 * halo), BF16),
            pltpu.SemaphoreType.DMA((groups,)),
        ],
        out_shape=jax.ShapeDtypeStruct((q * nocc, here), BF16),
        compiler_params=pltpu.CompilerParams(vmem_limit_bytes=50 * 2**20),
        cost_estimate=pl.CostEstimate(
            flops=2 * v_blocks.size * nocc, bytes_accessed=2 * v_blocks.size, transcendentals=0
        ),
    )(basis, pair_map, pair_count, own, pair, after, v_blocks)


def cuts_of(depth):
    cuts, start = [], 0
    for size in (256, 512):
        if start + size < depth:
            cuts.append((start, size))
            start += size
    while start < depth:
        size = min(768, depth - start)
        cuts.append((start, size))
        start += size
    return cuts


def product_kernel(step, kept, parts, adds, slab, aux_ref, basis_ref, virt_ref, *refs):
    half_refs, refs = refs[:parts], refs[parts:]
    add_refs, (out_ref, buf_ref, acc_ref, sems) = refs[: sum(adds)], refs[-4:]
    width = acc_ref.shape[1]
    chunk = basis_ref[0] ^ (2 * step + (0 if kept else 1))
    columns = pl.ds(pl.multiple_of(chunk * width, BB), width)
    cuts = cuts_of(virt_ref.shape[0])
    copies = [
        pltpu.make_async_copy(virt_ref.at[pl.ds(start, size), columns], buf_ref.at[pl.ds(start, size)], sems.at[i])
        for i, (start, size) in enumerate(cuts)
    ]
    for copy in copies:
        copy.start()
    for i, (start, size) in enumerate(cuts):
        copies[i].wait()
        rows = jnp.concatenate([ref[:, start : start + size] for ref in half_refs], axis=0)
        term = jnp.dot(rows, buf_ref[start : start + size], preferred_element_type=F32)
        if i == 0:
            at = 0
            for count in adds:
                term += jnp.concatenate([ref[...] for ref in add_refs[at : at + count]], axis=0).astype(F32)
                at += count
            acc_ref[...] = term
        elif i < len(cuts) - 1 or slab:
            acc_ref[...] += term
        else:
            out_ref[...] = (acc_ref[...] + term).astype(BF16)
    if slab:
        slabs = acc_ref.shape[0] // slab
        for s in range(slabs):
            rows = acc_ref[pl.ds(pl.multiple_of((aux_ref[0] ^ s) * slab, slab), slab), :]
            out_ref[:, s * slab : (s + 1) * slab] = rows.T.astype(BF16)


def product(scalars, virt, width, step, kept, parts, adds=(), after=(), slab=0):
    rows = sum(part.shape[0] for part in parts)
    depth = virt.shape[0]
    flat = [block for add in adds for block in add]
    shape = (width, rows) if slab else (rows, width)
    return pl.pallas_call(
        functools.partial(product_kernel, step, kept, len(parts), tuple(len(add) for add in adds), slab),
        in_specs=[SMEM, SMEM, HBM] + [VMEM] * (len(parts) + len(flat)) + [ANY] * len(after),
        out_specs=VMEM,
        scratch_shapes=[
            pltpu.VMEM((depth, width), BF16),
            pltpu.VMEM((rows, width), F32),
            pltpu.SemaphoreType.DMA((len(cuts_of(depth)),)),
        ],
        out_shape=jax.ShapeDtypeStruct(shape, BF16),
        compiler_params=pltpu.CompilerParams(vmem_limit_bytes=24 * 2**20),
        cost_estimate=pl.CostEstimate(
            flops=2 * rows * depth * width, bytes_accessed=2 * depth * width, transcendentals=0
        ),
    )(*scalars, virt, *parts, *flat, *after)


def local(v_blocks, pair_map, pair_count, occ_coef, virt_coef):
    peers = lax.axis_size("basis")
    slabs = lax.axis_size("aux")
    aux = lax.axis_index("aux").astype(jnp.int32)
    basis = lax.axis_index("basis").astype(jnp.int32)
    blocks = virt_coef.shape[0] // BB * peers
    halo = NEAR * BB

    even = basis % 2 == 0
    first, last = occ_coef[:, :halo], occ_coef[:, -halo:]
    pair = exchange(jnp.where(even, last, first), "basis", 1)
    ring = [(i, (i + 1 if i % 2 else i - 1) % peers) for i in range(peers)]
    after = lax.ppermute(jnp.where(even, first, last), "basis", ring)
    own = half_rows(basis.reshape(1), pair_map, pair_count, occ_coef, pair, after, v_blocks, blocks)
    width = virt_coef.shape[1] // peers
    groups = peers // 2
    steps = list(range(groups - 1, -1, -1))
    scalars = (aux.reshape(1), basis.reshape(1))
    chain = []

    def mult(step, kept, parts, adds=(), slab=0, after=()):
        out = product(scalars, virt_coef, width, step, kept, parts, adds, (*chain[-1:], *after), slab)
        chain.append(out)
        return out

    def send(step, parts, after=()):
        return exchange(mult(step, False, parts, after=after), "basis", 1)

    early = [own, exchange(own, "aux", 1)]
    far = [own]
    bit = slabs // 2
    while bit > 1:
        far += [exchange(rows, "aux", bit) for rows in far]
        bit //= 2
    far = far[1:]
    top, second, *others = range(groups - 1, -1, -1)
    received = {top: (send(top, early),)}
    received[second] = (send(second, early),)
    *far, _, _ = lax.optimization_barrier((*far, chain[-1], received[top][0]))
    late = [block for rows in far for block in (rows, exchange(rows, "aux", 1))]
    every = early + late
    received[top] += (send(top, late, received[top]),)
    received[second] += (send(second, late),)
    if groups == 4:
        received[1] = (send(1, every, received[2][:1]),)
        sent = mult(3, True, every, (received[3],))
        along = lambda pairs: [(2 * a + s, 2 * b + s) for a, b in pairs for s in (0, 1)]
        relayed = lax.ppermute(sent, "basis", along([(0, 1), (3, 2)]))
        arrived = [lax.ppermute(sent, "basis", along([(1, 2), (2, 1)]))]
        received[0] = (send(0, every, received[2][1:]),)
        sent = mult(2, True, every, (received[2], (relayed,)))
        arrived.append(exchange(sent, "basis", 4))
        sent = mult(1, True, every, (received[1],), after=arrived[:1])
        arrived.append(exchange(sent, "basis", 2))
    else:
        for m in others:
            received[m] = (send(m, every),)
        arrived = []
        for m in (top, second, *others[:-1]):
            sent = mult(m, True, every, (received[m],))
            arrived.append(exchange(sent, "basis", 2 * m))
    return mult(0, True, every, (received[0], *((array,) for array in arrived)), own.shape[0])


def solution(mesh):
    in_specs = (
        P("aux", "basis", None, None),
        P("aux", "basis", None),
        P("aux", "basis"),
        P(None, "basis"),
        P("basis", "aux"),
    )
    out_specs = P(("aux", "basis"), None)
    return jax.shard_map(local, mesh=mesh, in_specs=in_specs, out_specs=out_specs, check_vma=False)
```

```python
import functools

import jax
import jax.numpy as jnp
from jax import lax
from jax.experimental import pallas as pl
from jax.experimental.pallas import tpu as pltpu
from jax.sharding import PartitionSpec as P

BB = 128
NEAR = 8
F32 = jnp.float32
BF16 = jnp.bfloat16
VMEM = pl.BlockSpec(memory_space=pltpu.VMEM)
SMEM = pl.BlockSpec(memory_space=pltpu.SMEM)
HBM = pl.BlockSpec(memory_space=pltpu.HBM)
ANY = pl.BlockSpec(memory_space=pl.ANY)


def exchange(array, axis, bit):
    peers = lax.axis_size(axis)
    return lax.ppermute(array, axis, [(i, i ^ bit) for i in range(peers)])


def divisor(length, most):
    return max(d for d in range(1, most + 1) if length % d == 0)


def chunk_columns(basis, step, kept, width):
    chunk = basis ^ (2 * step + (0 if kept else 1))
    return pl.ds(pl.multiple_of(chunk * width, BB), width)


def half_kernel(
    groups, blocks, following, basis_ref, map_ref, count_ref, own_ref, pair_ref, next_ref, v_ref, virt_ref,
    out_ref, carry_ref, buf_ref, acc_ref, occ_ref, sems,
):
    q = v_ref.shape[0]
    nocc, here = own_ref.shape
    halo = pair_ref.shape[1]
    per = v_ref.shape[1] // groups
    blocks_here = here // BB
    first = basis_ref[0] * blocks_here
    copies = [
        pltpu.make_async_copy(v_ref.at[:, pl.ds(g * per, per)], buf_ref.at[g], sems.at[g]) for g in range(groups)
    ]
    columns = chunk_columns(basis_ref[0], *following, carry_ref.shape[1])
    carry = pltpu.make_async_copy(virt_ref.at[pl.ds(0, carry_ref.shape[0]), columns], carry_ref, sems.at[groups])
    for copy in (*copies, carry):
        copy.start()

    acc_ref[...] = jnp.zeros_like(acc_ref)
    odd = basis_ref[0] % 2
    occ_ref[:, halo : halo + here] = own_ref[...]
    occ_ref[:, pl.ds(pl.multiple_of((1 - odd) * (halo + here), BB), halo)] = pair_ref[...]
    occ_ref[:, pl.ds(pl.multiple_of(odd * (halo + here), BB), halo)] = next_ref[...]

    def picked(k):
        source = lax.rem(map_ref[0, k, 1] - first + NEAR + blocks, blocks)
        rows = occ_ref[:, pl.ds(pl.multiple_of(source * BB, BB), BB)]
        return jnp.where(k < count_ref[0, 0], rows, jnp.zeros_like(rows))

    for g in range(groups):
        copies[g].wait()
        sums = []
        for j in range(0, per, 2):
            k = g * per + j
            if j + 1 < per:
                one, two = picked(k), picked(k + 1)
                none = jnp.zeros_like(one)
                left = jnp.concatenate(
                    [jnp.concatenate([one, none], axis=1), jnp.concatenate([none, two], axis=1)], axis=0
                )
                right = jnp.concatenate([buf_ref[g, :, j], buf_ref[g, :, j + 1]], axis=-1).reshape(q * BB, 2 * BB)
            else:
                left, right = picked(k), buf_ref[g, :, j].reshape(q * BB, BB)
            sums.append(lax.dot_general(left, right, (((1,), (1,)), ((), ())), preferred_element_type=F32))
        for j in range(per):
            rows = sums[j // 2][(j % 2) * nocc : (j % 2 + 1) * nocc]
            target = pl.multiple_of((map_ref[0, g * per + j, 0] - first) * BB, BB)
            for p in range(q):
                acc_ref[p * nocc : (p + 1) * nocc, pl.ds(target, BB)] += rows[:, p * BB : (p + 1) * BB]
    out_ref[...] = acc_ref[...].astype(BF16)
    carry.wait()


def half_rows(basis, pair_map, pair_count, own, pair, after, v_blocks, virt, blocks, width, following):
    q, pairs = v_blocks.shape[:2]
    nocc, here = own.shape
    halo = pair.shape[1]
    groups = pairs // divisor(pairs, 8)
    return pl.pallas_call(
        functools.partial(half_kernel, groups, blocks, following),
        in_specs=[SMEM, SMEM, SMEM, VMEM, VMEM, VMEM, HBM, HBM],
        out_specs=[VMEM, VMEM],
        scratch_shapes=[
            pltpu.VMEM((groups, q, pairs // groups, BB, BB), BF16),
            pltpu.VMEM((q * nocc, here), F32),
            pltpu.VMEM((nocc, here + 2 * halo), BF16),
            pltpu.SemaphoreType.DMA((groups + 1,)),
        ],
        out_shape=[
            jax.ShapeDtypeStruct((q * nocc, here), BF16),
            jax.ShapeDtypeStruct((carried(virt.shape[0]), width), BF16),
        ],
        compiler_params=pltpu.CompilerParams(vmem_limit_bytes=50 * 2**20),
        cost_estimate=pl.CostEstimate(
            flops=2 * v_blocks.size * nocc, bytes_accessed=2 * v_blocks.size, transcendentals=0
        ),
    )(basis, pair_map, pair_count, own, pair, after, v_blocks, virt)


def carried(depth):
    return min(768, depth // 2)


def cuts_of(depth):
    start = carried(depth)
    return [(at, min(768, depth - at)) for at in range(start, depth, 768)]


def joined(refs):
    return jnp.concatenate([ref[...] for ref in refs], axis=0).astype(F32)


def product_kernel(step, kept, following, parts, adds, basis_ref, virt_ref, first_ref, *refs):
    half_refs, refs = refs[:parts], refs[parts:]
    add_refs = refs[: sum(adds)]
    out_ref, *carry_refs, buf_ref, acc_ref, sems = refs[-5 if following else -4 :]
    width = acc_ref.shape[1]
    columns = chunk_columns(basis_ref[0], step, kept, width)
    cuts = cuts_of(virt_ref.shape[0])
    copies = [
        pltpu.make_async_copy(
            virt_ref.at[pl.ds(start, size), columns], buf_ref.at[pl.ds(start - cuts[0][0], size)], sems.at[i]
        )
        for i, (start, size) in enumerate(cuts)
    ]
    for carry_ref in carry_refs:
        after = chunk_columns(basis_ref[0], *following, width)
        copies.append(
            pltpu.make_async_copy(
                virt_ref.at[pl.ds(0, carry_ref.shape[0]), after], carry_ref, sems.at[len(cuts)]
            )
        )
    for copy in copies:
        copy.start()

    def term(start, block):
        rows = jnp.concatenate([ref[:, start : start + block.shape[0]] for ref in half_refs], axis=0)
        return jnp.dot(rows, block, preferred_element_type=F32)

    total = term(0, first_ref[...])
    at = 0
    for count in adds:
        total += joined(add_refs[at : at + count])
        at += count
    acc_ref[...] = total
    for i, (start, size) in enumerate(cuts):
        copies[i].wait()
        total = acc_ref[...] + term(start, buf_ref[start - cuts[0][0] : start - cuts[0][0] + size])
        if i < len(cuts) - 1:
            acc_ref[...] = total
        else:
            out_ref[...] = total.astype(out_ref.dtype)
    for copy in copies[len(cuts) :]:
        copy.wait()


def product(basis, virt, first, step, kept, following, parts, adds=(), after=(), dtype=BF16):
    rows = sum(part.shape[0] for part in parts)
    depth, width = virt.shape[0], first.shape[1]
    flat = [block for add in adds for block in add]
    shapes = [jax.ShapeDtypeStruct((rows, width), dtype)]
    if following:
        shapes.append(jax.ShapeDtypeStruct(first.shape, BF16))
    return pl.pallas_call(
        functools.partial(product_kernel, step, kept, following, len(parts), tuple(len(add) for add in adds)),
        in_specs=[SMEM, HBM] + [VMEM] * (1 + len(parts) + len(flat)) + [ANY] * len(after),
        out_specs=[VMEM] * len(shapes),
        scratch_shapes=[
            pltpu.VMEM((depth - first.shape[0], width), BF16),
            pltpu.VMEM((rows, width), F32),
            pltpu.SemaphoreType.DMA((len(cuts_of(depth)) + 1,)),
        ],
        out_shape=shapes,
        compiler_params=pltpu.CompilerParams(vmem_limit_bytes=24 * 2**20),
        cost_estimate=pl.CostEstimate(
            flops=2 * rows * depth * width, bytes_accessed=2 * depth * width, transcendentals=0
        ),
    )(basis, virt, first, *parts, *flat, *after)


def finish_kernel(slab, adds, aux_ref, total_ref, *refs):
    add_refs, (out_ref, acc_ref) = refs[: sum(adds)], refs[-2:]
    total = total_ref[...]
    at = 0
    for count in adds:
        total += joined(add_refs[at : at + count])
        at += count
    acc_ref[...] = total
    for s in range(acc_ref.shape[0] // slab):
        rows = acc_ref[pl.ds(pl.multiple_of((aux_ref[0] ^ s) * slab, slab), slab), :]
        out_ref[:, s * slab : (s + 1) * slab] = rows.T.astype(BF16)


def finish(aux, total, adds, slab):
    flat = [block for add in adds for block in add]
    return pl.pallas_call(
        functools.partial(finish_kernel, slab, tuple(len(add) for add in adds)),
        in_specs=[SMEM] + [VMEM] * (1 + len(flat)),
        out_specs=VMEM,
        scratch_shapes=[pltpu.VMEM(total.shape, F32)],
        out_shape=jax.ShapeDtypeStruct(total.shape[::-1], BF16),
        compiler_params=pltpu.CompilerParams(vmem_limit_bytes=24 * 2**20),
    )(aux, total, *flat)


def local(v_blocks, pair_map, pair_count, occ_coef, virt_coef):
    peers = lax.axis_size("basis")
    slabs = lax.axis_size("aux")
    aux = lax.axis_index("aux").astype(jnp.int32)
    basis = lax.axis_index("basis").astype(jnp.int32)
    blocks = virt_coef.shape[0] // BB * peers
    halo = NEAR * BB

    even = basis % 2 == 0
    first, last = occ_coef[:, :halo], occ_coef[:, -halo:]
    pair = exchange(jnp.where(even, last, first), "basis", 1)
    ring = [(i, (i + 1 if i % 2 else i - 1) % peers) for i in range(peers)]
    after = lax.ppermute(jnp.where(even, first, last), "basis", ring)
    width = virt_coef.shape[1] // peers
    groups = peers // 2
    top, second, *others = range(groups - 1, -1, -1)
    sends = [(m, False) for m in (top, second)]
    keeps = [(m, True) for m in (top, second, *others)]
    if groups == 4:
        order = [*sends, keeps[0], *sends, (1, False), keeps[0], (0, False), keeps[1], keeps[3], keeps[2]]
    else:
        order = [*sends, *sends, *((m, False) for m in others), *keeps]
    number = basis.reshape(1)
    own, first = half_rows(
        number, pair_map, pair_count, occ_coef, pair, after, v_blocks, virt_coef, blocks, width, order[0]
    )
    carry = [first]

    def mult(step, kept, parts, adds=(), after=(), dtype=BF16):
        assert order.pop(0) == (step, kept)
        following = order[0] if order else None
        out, *carry[:] = product(number, virt_coef, carry[0], step, kept, following, parts, adds, after, dtype)
        return out

    def send(step, parts, after=()):
        return exchange(mult(step, False, parts, after=after), "basis", 1)

    early = [own, exchange(own, "aux", 1)]
    far = [own]
    bit = slabs // 2
    while bit > 1:
        far += [exchange(rows, "aux", bit) for rows in far]
        bit //= 2
    far = far[1:]
    received = {top: (send(top, early),)}
    received[second] = (send(second, early),)
    along = lambda pairs: [(2 * a + s, 2 * b + s) for a, b in pairs for s in (0, 1)]
    relayed, inner = [], []

    def outer(parts, add):
        sent = mult(3, True, parts, (add,))
        relayed.append(lax.ppermute(sent, "basis", along([(0, 1), (3, 2)])))
        inner.append(lax.ppermute(sent, "basis", along([(1, 2), (2, 1)])))

    if groups == 4:
        outer(early, received[3])
    *far, _ = lax.optimization_barrier((*far, carry[0]))
    late = [block for rows in far for block in (rows, exchange(rows, "aux", 1))]
    every = early + late
    received[top] += (send(top, late, received[top]),)
    received[second] += (send(second, late),)
    if groups == 4:
        received[1] = (send(1, every, received[2][:1]),)
        outer(late, received[3][1:])
        received[0] = (send(0, every),)
        part = mult(2, True, every, (received[2],), dtype=F32)
        total = mult(0, True, every, dtype=F32)
        sent = (part + jnp.concatenate(relayed, axis=0).astype(F32)).astype(BF16)
        third = exchange(sent, "basis", 4)
        sent = mult(1, True, every, (received[1],), after=inner)
        adds = (received[0], tuple(inner), (third,), (exchange(sent, "basis", 2),))
    else:
        for m in others:
            received[m] = (send(m, every),)
        adds = (received[0],)
        for m in (top, second, *others[:-1]):
            sent = mult(m, True, every, (received[m],))
            adds += ((exchange(sent, "basis", 2 * m),),)
        total = mult(0, True, every, dtype=F32)
    return finish(aux.reshape(1), total, adds, own.shape[0])


def solution(mesh):
    in_specs = (
        P("aux", "basis", None, None),
        P("aux", "basis", None),
        P("aux", "basis"),
        P(None, "basis"),
        P("basis", "aux"),
    )
    out_specs = P(("aux", "basis"), None)
    return jax.shard_map(local, mesh=mesh, in_specs=in_specs, out_specs=out_specs, check_vma=False)
```

```python
import functools

import jax
import jax.numpy as jnp
from jax import lax
from jax.experimental import pallas as pl
from jax.experimental.pallas import tpu as pltpu
from jax.sharding import PartitionSpec as P

BB = 128
NEAR = 8
F32 = jnp.float32
BF16 = jnp.bfloat16
VMEM = pl.BlockSpec(memory_space=pltpu.VMEM)
SMEM = pl.BlockSpec(memory_space=pltpu.SMEM)
HBM = pl.BlockSpec(memory_space=pltpu.HBM)
ANY = pl.BlockSpec(memory_space=pl.ANY)


def exchange(array, axis, bit):
    peers = lax.axis_size(axis)
    return lax.ppermute(array, axis, [(i, i ^ bit) for i in range(peers)])


def divisor(length, most):
    return max(d for d in range(1, most + 1) if length % d == 0)


def chunk_columns(basis, step, kept, width):
    chunk = basis ^ (2 * step + (0 if kept else 1))
    return pl.ds(pl.multiple_of(chunk * width, BB), width)


def half_kernel(
    groups, blocks, following, basis_ref, map_ref, count_ref, table_ref, pair_ref, next_ref, v_ref, virt_ref,
    out_ref, carry_ref, buf_ref, acc_ref, occ_ref, sems,
):
    q = v_ref.shape[0]
    nocc, halo = pair_ref.shape
    here = table_ref.shape[1] - 2 * halo
    per = v_ref.shape[1] // groups
    blocks_here = here // BB
    first = basis_ref[0] * blocks_here
    copies = [
        pltpu.make_async_copy(v_ref.at[:, pl.ds(g * per, per)], buf_ref.at[g], sems.at[g]) for g in range(groups)
    ]
    columns = chunk_columns(basis_ref[0], *following, carry_ref.shape[1])
    carry = pltpu.make_async_copy(virt_ref.at[pl.ds(0, carry_ref.shape[0]), columns], carry_ref, sems.at[groups])
    for copy in (*copies, carry):
        copy.start()

    acc_ref[...] = jnp.zeros_like(acc_ref)
    odd = basis_ref[0] % 2
    occ_ref[...] = table_ref[...]
    occ_ref[:, pl.ds(pl.multiple_of((1 - odd) * (halo + here), BB), halo)] = pair_ref[...]
    occ_ref[:, pl.ds(pl.multiple_of(odd * (halo + here), BB), halo)] = next_ref[...]

    def picked(k):
        source = lax.rem(map_ref[0, k, 1] - first + NEAR + blocks, blocks)
        rows = occ_ref[:, pl.ds(pl.multiple_of(source * BB, BB), BB)]
        return jnp.where(k < count_ref[0, 0], rows, jnp.zeros_like(rows))

    for g in range(groups):
        copies[g].wait()
        sums = []
        for j in range(0, per, 2):
            k = g * per + j
            if j + 1 < per:
                one, two = picked(k), picked(k + 1)
                none = jnp.zeros_like(one)
                left = jnp.concatenate(
                    [jnp.concatenate([one, none], axis=1), jnp.concatenate([none, two], axis=1)], axis=0
                )
                right = jnp.concatenate([buf_ref[g, :, j], buf_ref[g, :, j + 1]], axis=-1).reshape(q * BB, 2 * BB)
            else:
                left, right = picked(k), buf_ref[g, :, j].reshape(q * BB, BB)
            sums.append(lax.dot_general(left, right, (((1,), (1,)), ((), ())), preferred_element_type=F32))
        for j in range(per):
            rows = sums[j // 2][(j % 2) * nocc : (j % 2 + 1) * nocc]
            target = pl.multiple_of((map_ref[0, g * per + j, 0] - first) * BB, BB)
            for p in range(q):
                acc_ref[p * nocc : (p + 1) * nocc, pl.ds(target, BB)] += rows[:, p * BB : (p + 1) * BB]
    out_ref[...] = acc_ref[...].astype(BF16)
    carry.wait()


def half_rows(basis, pair_map, pair_count, table, pair, after, v_blocks, virt, blocks, width, following):
    q, pairs = v_blocks.shape[:2]
    nocc, halo = pair.shape
    here = table.shape[1] - 2 * halo
    groups = pairs // divisor(pairs, 4)
    return pl.pallas_call(
        functools.partial(half_kernel, groups, blocks, following),
        in_specs=[SMEM, SMEM, SMEM, VMEM, VMEM, VMEM, HBM, HBM],
        out_specs=[VMEM, VMEM],
        scratch_shapes=[
            pltpu.VMEM((groups, q, pairs // groups, BB, BB), BF16),
            pltpu.VMEM((q * nocc, here), F32),
            pltpu.VMEM((nocc, here + 2 * halo), BF16),
            pltpu.SemaphoreType.DMA((groups + 1,)),
        ],
        out_shape=[
            jax.ShapeDtypeStruct((q * nocc, here), BF16),
            jax.ShapeDtypeStruct((carried(virt.shape[0]), width), BF16),
        ],
        compiler_params=pltpu.CompilerParams(vmem_limit_bytes=50 * 2**20),
        cost_estimate=pl.CostEstimate(
            flops=2 * v_blocks.size * nocc, bytes_accessed=2 * v_blocks.size, transcendentals=0
        ),
    )(basis, pair_map, pair_count, table, pair, after, v_blocks, virt)


def carried(depth):
    return min(768, depth // 2)


def cuts_of(depth):
    start = carried(depth)
    return [(at, min(768, depth - at)) for at in range(start, depth, 768)]


def joined(refs):
    return jnp.concatenate([ref[...] for ref in refs], axis=0).astype(F32)


def product_kernel(step, kept, following, parts, adds, basis_ref, virt_ref, first_ref, *refs):
    half_refs, refs = refs[:parts], refs[parts:]
    add_refs = refs[: sum(adds)]
    out_ref, *carry_refs, buf_ref, acc_ref, sems = refs[-5 if following else -4 :]
    width = acc_ref.shape[1]
    columns = chunk_columns(basis_ref[0], step, kept, width)
    cuts = cuts_of(virt_ref.shape[0])
    copies = [
        pltpu.make_async_copy(
            virt_ref.at[pl.ds(start, size), columns], buf_ref.at[pl.ds(start - cuts[0][0], size)], sems.at[i]
        )
        for i, (start, size) in enumerate(cuts)
    ]
    for carry_ref in carry_refs:
        after = chunk_columns(basis_ref[0], *following, width)
        copies.append(
            pltpu.make_async_copy(
                virt_ref.at[pl.ds(0, carry_ref.shape[0]), after], carry_ref, sems.at[len(cuts)]
            )
        )
    for copy in copies:
        copy.start()

    def term(start, block):
        rows = jnp.concatenate([ref[:, start : start + block.shape[0]] for ref in half_refs], axis=0)
        return jnp.dot(rows, block, preferred_element_type=F32)

    total = term(0, first_ref[...])
    at = 0
    for count in adds:
        total += joined(add_refs[at : at + count])
        at += count
    acc_ref[...] = total
    for i, (start, size) in enumerate(cuts):
        copies[i].wait()
        total = acc_ref[...] + term(start, buf_ref[start - cuts[0][0] : start - cuts[0][0] + size])
        if i < len(cuts) - 1:
            acc_ref[...] = total
        else:
            out_ref[...] = total.astype(out_ref.dtype)
    for copy in copies[len(cuts) :]:
        copy.wait()


def product(basis, virt, first, step, kept, following, parts, adds=(), after=(), dtype=BF16):
    rows = sum(part.shape[0] for part in parts)
    depth, width = virt.shape[0], first.shape[1]
    flat = [block for add in adds for block in add]
    shapes = [jax.ShapeDtypeStruct((rows, width), dtype)]
    if following:
        shapes.append(jax.ShapeDtypeStruct(first.shape, BF16))
    return pl.pallas_call(
        functools.partial(product_kernel, step, kept, following, len(parts), tuple(len(add) for add in adds)),
        in_specs=[SMEM, HBM] + [VMEM] * (1 + len(parts) + len(flat)) + [ANY] * len(after),
        out_specs=[VMEM] * len(shapes),
        scratch_shapes=[
            pltpu.VMEM((depth - first.shape[0], width), BF16),
            pltpu.VMEM((rows, width), F32),
            pltpu.SemaphoreType.DMA((len(cuts_of(depth)) + 1,)),
        ],
        out_shape=shapes,
        compiler_params=pltpu.CompilerParams(vmem_limit_bytes=24 * 2**20),
        cost_estimate=pl.CostEstimate(
            flops=2 * rows * depth * width, bytes_accessed=2 * depth * width, transcendentals=0
        ),
    )(basis, virt, first, *parts, *flat, *after)


def finish_kernel(slab, adds, aux_ref, total_ref, *refs):
    add_refs, (out_ref, acc_ref) = refs[: sum(adds)], refs[-2:]
    total = total_ref[...]
    at = 0
    for count in adds:
        total += joined(add_refs[at : at + count])
        at += count
    acc_ref[...] = total
    for s in range(acc_ref.shape[0] // slab):
        rows = acc_ref[pl.ds(pl.multiple_of((aux_ref[0] ^ s) * slab, slab), slab), :]
        out_ref[:, s * slab : (s + 1) * slab] = rows.T.astype(BF16)


def finish(aux, total, adds, slab):
    flat = [block for add in adds for block in add]
    return pl.pallas_call(
        functools.partial(finish_kernel, slab, tuple(len(add) for add in adds)),
        in_specs=[SMEM] + [VMEM] * (1 + len(flat)),
        out_specs=VMEM,
        scratch_shapes=[pltpu.VMEM(total.shape, F32)],
        out_shape=jax.ShapeDtypeStruct(total.shape[::-1], BF16),
        compiler_params=pltpu.CompilerParams(vmem_limit_bytes=24 * 2**20),
    )(aux, total, *flat)


def local(v_blocks, pair_map, pair_count, occ_coef, virt_coef):
    peers = lax.axis_size("basis")
    slabs = lax.axis_size("aux")
    aux = lax.axis_index("aux").astype(jnp.int32)
    basis = lax.axis_index("basis").astype(jnp.int32)
    blocks = virt_coef.shape[0] // BB * peers
    halo = NEAR * BB

    even = basis % 2 == 0
    first, last = occ_coef[:, :halo], occ_coef[:, -halo:]
    pair = exchange(jnp.where(even, last, first), "basis", 1)
    ring = [(i, (i + 1 if i % 2 else i - 1) % peers) for i in range(peers)]
    after = lax.ppermute(jnp.where(even, first, last), "basis", ring)
    table = jnp.pad(occ_coef, ((0, 0), (halo, halo)))
    width = virt_coef.shape[1] // peers
    groups = peers // 2
    top, second, *others = range(groups - 1, -1, -1)
    sends = [(m, False) for m in (top, second)]
    keeps = [(m, True) for m in (top, second, *others)]
    if groups == 4:
        order = [*sends, *sends, (1, False), keeps[0], (0, False), keeps[1], keeps[3], keeps[2]]
    else:
        order = [*sends, *sends, *((m, False) for m in others), *keeps]
    number = basis.reshape(1)
    own, first = half_rows(
        number, pair_map, pair_count, table, pair, after, v_blocks, virt_coef, blocks, width, order[0]
    )
    carry = [first]

    def mult(step, kept, parts, adds=(), after=(), dtype=BF16):
        assert order.pop(0) == (step, kept)
        following = order[0] if order else None
        out, *carry[:] = product(number, virt_coef, carry[0], step, kept, following, parts, adds, after, dtype)
        return out

    def send(step, parts, after=()):
        return exchange(mult(step, False, parts, after=after), "basis", 1)

    early = [own, exchange(own, "aux", 1)]
    far = [own]
    bit = slabs // 2
    while bit > 1:
        far += [exchange(rows, "aux", bit) for rows in far]
        bit //= 2
    far = far[1:]
    received = {top: (send(top, early),)}
    received[second] = (send(second, early),)
    *far, _, _ = lax.optimization_barrier((*far, carry[0], received[top][0]))
    late = [block for rows in far for block in (rows, exchange(rows, "aux", 1))]
    every = early + late
    received[top] += (send(top, late),)
    received[second] += (send(second, late),)
    if groups == 4:
        received[1] = (send(1, every, received[2][:1]),)
        sent = mult(3, True, every, (received[3],))
        along = lambda pairs: [(2 * a + s, 2 * b + s) for a, b in pairs for s in (0, 1)]
        relayed = lax.ppermute(sent, "basis", along([(0, 1), (3, 2)]))
        inner = lax.ppermute(sent, "basis", along([(1, 2), (2, 1)]))
        received[0] = (send(0, every),)
        part = mult(2, True, every, (received[2],), dtype=F32)
        total = mult(0, True, every, dtype=F32)
        sent = (part + relayed.astype(F32)).astype(BF16)
        third = exchange(sent, "basis", 4)
        sent = mult(1, True, every, (received[1],), after=(inner,))
        adds = (received[0], (inner,), (third,), (exchange(sent, "basis", 2),))
    else:
        for m in others:
            received[m] = (send(m, every),)
        adds = (received[0],)
        for m in (top, second, *others[:-1]):
            sent = mult(m, True, every, (received[m],))
            adds += ((exchange(sent, "basis", 2 * m),),)
        total = mult(0, True, every, dtype=F32)
    return finish(aux.reshape(1), total, adds, own.shape[0])


def solution(mesh):
    in_specs = (
        P("aux", "basis", None, None),
        P("aux", "basis", None),
        P("aux", "basis"),
        P(None, "basis"),
        P("basis", "aux"),
    )
    out_specs = P(("aux", "basis"), None)
    return jax.shard_map(local, mesh=mesh, in_specs=in_specs, out_specs=out_specs, check_vma=False)
```

```python
import functools

import jax
import jax.numpy as jnp
from jax import lax
from jax.experimental import pallas as pl
from jax.experimental.pallas import tpu as pltpu
from jax.sharding import PartitionSpec as P

BB = 128
NEAR = 8
F32 = jnp.float32
BF16 = jnp.bfloat16
VMEM = pl.BlockSpec(memory_space=pltpu.VMEM)
SMEM = pl.BlockSpec(memory_space=pltpu.SMEM)
HBM = pl.BlockSpec(memory_space=pltpu.HBM)
ANY = pl.BlockSpec(memory_space=pl.ANY)


def exchange(array, axis, bit):
    peers = lax.axis_size(axis)
    return lax.ppermute(array, axis, [(i, i ^ bit) for i in range(peers)])


def divisor(length, most):
    return max(d for d in range(1, most + 1) if length % d == 0)


def chunk_columns(basis, step, kept, width):
    chunk = basis ^ (2 * step + (0 if kept else 1))
    return pl.ds(pl.multiple_of(chunk * width, BB), width)


def half_kernel(
    groups, blocks, following, basis_ref, map_ref, count_ref, table_ref, pair_ref, next_ref, v_ref, virt_ref,
    out_ref, carry_ref, buf_ref, acc_ref, occ_ref, sems,
):
    q = v_ref.shape[0]
    nocc, halo = pair_ref.shape
    here = table_ref.shape[1] - 2 * halo
    per = v_ref.shape[1] // groups
    blocks_here = here // BB
    first = basis_ref[0] * blocks_here
    copies = [
        pltpu.make_async_copy(v_ref.at[:, pl.ds(g * per, per)], buf_ref.at[g], sems.at[g]) for g in range(groups)
    ]
    columns = chunk_columns(basis_ref[0], *following, carry_ref.shape[1])
    carry = pltpu.make_async_copy(virt_ref.at[pl.ds(0, carry_ref.shape[0]), columns], carry_ref, sems.at[groups])
    for copy in (*copies, carry):
        copy.start()

    acc_ref[...] = jnp.zeros_like(acc_ref)
    odd = basis_ref[0] % 2
    occ_ref[...] = table_ref[...]
    occ_ref[:, pl.ds(pl.multiple_of((1 - odd) * (halo + here), BB), halo)] = pair_ref[...]
    occ_ref[:, pl.ds(pl.multiple_of(odd * (halo + here), BB), halo)] = next_ref[...]

    def picked(k):
        source = lax.rem(map_ref[0, k, 1] - first + NEAR + blocks, blocks)
        rows = occ_ref[:, pl.ds(pl.multiple_of(source * BB, BB), BB)]
        return jnp.where(k < count_ref[0, 0], rows, jnp.zeros_like(rows))

    for g in range(groups):
        copies[g].wait()
        sums = []
        for j in range(0, per, 2):
            k = g * per + j
            if j + 1 < per:
                one, two = picked(k), picked(k + 1)
                none = jnp.zeros_like(one)
                left = jnp.concatenate(
                    [jnp.concatenate([one, none], axis=1), jnp.concatenate([none, two], axis=1)], axis=0
                )
                right = jnp.concatenate([buf_ref[g, :, j], buf_ref[g, :, j + 1]], axis=-1).reshape(q * BB, 2 * BB)
            else:
                left, right = picked(k), buf_ref[g, :, j].reshape(q * BB, BB)
            sums.append(lax.dot_general(left, right, (((1,), (1,)), ((), ())), preferred_element_type=F32))
        for j in range(per):
            rows = sums[j // 2][(j % 2) * nocc : (j % 2 + 1) * nocc]
            target = pl.multiple_of((map_ref[0, g * per + j, 0] - first) * BB, BB)
            for p in range(q):
                acc_ref[p * nocc : (p + 1) * nocc, pl.ds(target, BB)] += rows[:, p * BB : (p + 1) * BB]
    out_ref[...] = acc_ref[...].astype(BF16)
    carry.wait()


def half_rows(basis, pair_map, pair_count, table, pair, after, v_blocks, virt, blocks, width, following):
    q, pairs = v_blocks.shape[:2]
    nocc, halo = pair.shape
    here = table.shape[1] - 2 * halo
    groups = pairs // divisor(pairs, 4)
    return pl.pallas_call(
        functools.partial(half_kernel, groups, blocks, following),
        in_specs=[SMEM, SMEM, SMEM, VMEM, VMEM, VMEM, HBM, HBM],
        out_specs=[VMEM, VMEM],
        scratch_shapes=[
            pltpu.VMEM((groups, q, pairs // groups, BB, BB), BF16),
            pltpu.VMEM((q * nocc, here), F32),
            pltpu.VMEM((nocc, here + 2 * halo), BF16),
            pltpu.SemaphoreType.DMA((groups + 1,)),
        ],
        out_shape=[
            jax.ShapeDtypeStruct((q * nocc, here), BF16),
            jax.ShapeDtypeStruct((carried(virt.shape[0]), width), BF16),
        ],
        compiler_params=pltpu.CompilerParams(vmem_limit_bytes=50 * 2**20),
        cost_estimate=pl.CostEstimate(
            flops=2 * v_blocks.size * nocc, bytes_accessed=2 * v_blocks.size, transcendentals=0
        ),
    )(basis, pair_map, pair_count, table, pair, after, v_blocks, virt)


def carried(depth):
    return min(768, depth // 2)


def cuts_of(depth):
    start = carried(depth)
    return [(at, min(768, depth - at)) for at in range(start, depth, 768)]


def joined(refs):
    return jnp.concatenate([ref[...] for ref in refs], axis=0).astype(F32)


def product_kernel(step, kept, following, parts, adds, basis_ref, virt_ref, first_ref, *refs):
    half_refs, refs = refs[:parts], refs[parts:]
    add_refs = refs[: sum(adds)]
    out_ref, *carry_refs, buf_ref, acc_ref, sems = refs[-5 if following else -4 :]
    width = acc_ref.shape[1]
    columns = chunk_columns(basis_ref[0], step, kept, width)
    cuts = cuts_of(virt_ref.shape[0])
    copies = [
        pltpu.make_async_copy(
            virt_ref.at[pl.ds(start, size), columns], buf_ref.at[pl.ds(start - cuts[0][0], size)], sems.at[i]
        )
        for i, (start, size) in enumerate(cuts)
    ]
    for carry_ref in carry_refs:
        after = chunk_columns(basis_ref[0], *following, width)
        copies.append(
            pltpu.make_async_copy(
                virt_ref.at[pl.ds(0, carry_ref.shape[0]), after], carry_ref, sems.at[len(cuts)]
            )
        )
    for copy in copies:
        copy.start()

    def term(start, block):
        rows = jnp.concatenate([ref[:, start : start + block.shape[0]] for ref in half_refs], axis=0)
        return jnp.dot(rows, block, preferred_element_type=F32)

    total = term(0, first_ref[...])
    at = 0
    for count in adds:
        total += joined(add_refs[at : at + count])
        at += count
    acc_ref[...] = total
    for i, (start, size) in enumerate(cuts):
        copies[i].wait()
        total = acc_ref[...] + term(start, buf_ref[start - cuts[0][0] : start - cuts[0][0] + size])
        if i < len(cuts) - 1:
            acc_ref[...] = total
        else:
            out_ref[...] = total.astype(out_ref.dtype)
    for copy in copies[len(cuts) :]:
        copy.wait()


def product(basis, virt, first, step, kept, following, parts, adds=(), after=(), dtype=BF16):
    rows = sum(part.shape[0] for part in parts)
    depth, width = virt.shape[0], first.shape[1]
    flat = [block for add in adds for block in add]
    shapes = [jax.ShapeDtypeStruct((rows, width), dtype)]
    if following:
        shapes.append(jax.ShapeDtypeStruct(first.shape, BF16))
    return pl.pallas_call(
        functools.partial(product_kernel, step, kept, following, len(parts), tuple(len(add) for add in adds)),
        in_specs=[SMEM, HBM] + [VMEM] * (1 + len(parts) + len(flat)) + [ANY] * len(after),
        out_specs=[VMEM] * len(shapes),
        scratch_shapes=[
            pltpu.VMEM((depth - first.shape[0], width), BF16),
            pltpu.VMEM((rows, width), F32),
            pltpu.SemaphoreType.DMA((len(cuts_of(depth)) + 1,)),
        ],
        out_shape=shapes,
        compiler_params=pltpu.CompilerParams(vmem_limit_bytes=24 * 2**20),
        cost_estimate=pl.CostEstimate(
            flops=2 * rows * depth * width, bytes_accessed=2 * depth * width, transcendentals=0
        ),
    )(basis, virt, first, *parts, *flat, *after)


def finish_kernel(slab, adds, aux_ref, total_ref, *refs):
    add_refs, (out_ref, acc_ref) = refs[: sum(adds)], refs[-2:]
    total = total_ref[...]
    at = 0
    for count in adds:
        total += joined(add_refs[at : at + count])
        at += count
    acc_ref[...] = total
    for s in range(acc_ref.shape[0] // slab):
        rows = acc_ref[pl.ds(pl.multiple_of((aux_ref[0] ^ s) * slab, slab), slab), :]
        out_ref[:, s * slab : (s + 1) * slab] = rows.T.astype(BF16)


def finish(aux, total, adds, slab):
    flat = [block for add in adds for block in add]
    return pl.pallas_call(
        functools.partial(finish_kernel, slab, tuple(len(add) for add in adds)),
        in_specs=[SMEM] + [VMEM] * (1 + len(flat)),
        out_specs=VMEM,
        scratch_shapes=[pltpu.VMEM(total.shape, F32)],
        out_shape=jax.ShapeDtypeStruct(total.shape[::-1], BF16),
        compiler_params=pltpu.CompilerParams(vmem_limit_bytes=24 * 2**20),
    )(aux, total, *flat)


def local(v_blocks, pair_map, pair_count, occ_coef, virt_coef):
    peers = lax.axis_size("basis")
    slabs = lax.axis_size("aux")
    aux = lax.axis_index("aux").astype(jnp.int32)
    basis = lax.axis_index("basis").astype(jnp.int32)
    blocks = virt_coef.shape[0] // BB * peers
    halo = NEAR * BB

    even = basis % 2 == 0
    first, last = occ_coef[:, :halo], occ_coef[:, -halo:]
    pair = exchange(jnp.where(even, last, first), "basis", 1)
    ring = [(i, (i + 1 if i % 2 else i - 1) % peers) for i in range(peers)]
    after = lax.ppermute(jnp.where(even, first, last), "basis", ring)
    table = jnp.pad(occ_coef, ((0, 0), (halo, halo)))
    width = virt_coef.shape[1] // peers
    groups = peers // 2
    top, second, *others = range(groups - 1, -1, -1)
    sends = [(m, False) for m in (top, second)]
    keeps = [(m, True) for m in (top, second, *others)]
    if groups == 4:
        order = [*sends, *sends, keeps[0], (1, False), keeps[1], (0, False), keeps[2], keeps[3]]
    else:
        order = [*sends, *sends, *((m, False) for m in others), *keeps]
    number = basis.reshape(1)
    own, first = half_rows(
        number, pair_map, pair_count, table, pair, after, v_blocks, virt_coef, blocks, width, order[0]
    )
    carry = [first]

    def mult(step, kept, parts, adds=(), after=(), dtype=BF16):
        assert order.pop(0) == (step, kept)
        following = order[0] if order else None
        out, *carry[:] = product(number, virt_coef, carry[0], step, kept, following, parts, adds, after, dtype)
        return out

    def send(step, parts, after=()):
        return exchange(mult(step, False, parts, after=after), "basis", 1)

    early = [own, exchange(own, "aux", 1)]
    far = [own]
    bit = slabs // 2
    while bit > 1:
        far += [exchange(rows, "aux", bit) for rows in far]
        bit //= 2
    far = far[1:]
    received = {top: (send(top, early),)}
    received[second] = (send(second, early),)
    *far, _, _ = lax.optimization_barrier((*far, carry[0], received[top][0]))
    late = [block for rows in far for block in (rows, exchange(rows, "aux", 1))]
    every = early + late
    received[top] += (send(top, late),)
    received[second] += (send(second, late),)
    if groups == 4:
        along = lambda pairs: [(2 * a + s, 2 * b + s) for a, b in pairs for s in (0, 1)]
        sent = mult(3, True, every, (received[3],), after=received[2][:1])
        relayed = lax.ppermute(sent, "basis", along([(0, 1), (3, 2)]))
        inner = lax.ppermute(sent, "basis", along([(1, 2), (2, 1)]))
        received[1] = (send(1, every),)
        sent = mult(2, True, every, (received[2],))
        outer = lax.ppermute(sent, "basis", along([(0, 2), (3, 1)]))
        received[0] = (send(0, every),)
        both = (sent.astype(F32) + relayed.astype(F32)).astype(BF16)
        third = lax.ppermute(both, "basis", along([(1, 3), (2, 0)]))
        sent = mult(1, True, every, (received[1],), after=(both, inner))
        fourth = exchange(sent, "basis", 2)
        total = mult(0, True, every, dtype=F32)
        adds = (received[0], (inner,), (outer,), (third,), (fourth,))
    else:
        for m in others:
            received[m] = (send(m, every),)
        adds = (received[0],)
        for m in (top, second, *others[:-1]):
            sent = mult(m, True, every, (received[m],))
            adds += ((exchange(sent, "basis", 2 * m),),)
        total = mult(0, True, every, dtype=F32)
    return finish(aux.reshape(1), total, adds, own.shape[0])


def solution(mesh):
    in_specs = (
        P("aux", "basis", None, None),
        P("aux", "basis", None),
        P("aux", "basis"),
        P(None, "basis"),
        P("basis", "aux"),
    )
    out_specs = P(("aux", "basis"), None)
    return jax.shard_map(local, mesh=mesh, in_specs=in_specs, out_specs=out_specs, check_vma=False)
```

```python
import functools

import jax
import jax.numpy as jnp
from jax import lax
from jax.experimental import pallas as pl
from jax.experimental.pallas import tpu as pltpu
from jax.sharding import PartitionSpec as P

BB = 128
NEAR = 8
F32 = jnp.float32
BF16 = jnp.bfloat16
VMEM = pl.BlockSpec(memory_space=pltpu.VMEM)
SMEM = pl.BlockSpec(memory_space=pltpu.SMEM)
HBM = pl.BlockSpec(memory_space=pltpu.HBM)
ANY = pl.BlockSpec(memory_space=pl.ANY)


def exchange(array, axis, bit):
    peers = lax.axis_size(axis)
    return lax.ppermute(array, axis, [(i, i ^ bit) for i in range(peers)])


def divisor(length, most):
    return max(d for d in range(1, most + 1) if length % d == 0)


def chunk_columns(basis, step, kept, width):
    chunk = basis ^ (2 * step + (0 if kept else 1))
    return pl.ds(pl.multiple_of(chunk * width, BB), width)


def half_kernel(
    groups, blocks, following, basis_ref, map_ref, count_ref, table_ref, pair_ref, next_ref, v_ref, virt_ref,
    out_ref, carry_ref, buf_ref, acc_ref, occ_ref, sems,
):
    q = v_ref.shape[0]
    nocc, halo = pair_ref.shape
    here = table_ref.shape[1] - 2 * halo
    per = v_ref.shape[1] // groups
    blocks_here = here // BB
    first = basis_ref[0] * blocks_here
    copies = [
        pltpu.make_async_copy(v_ref.at[:, pl.ds(g * per, per)], buf_ref.at[g], sems.at[g]) for g in range(groups)
    ]
    columns = chunk_columns(basis_ref[0], *following, carry_ref.shape[1])
    carry = pltpu.make_async_copy(virt_ref.at[pl.ds(0, carry_ref.shape[0]), columns], carry_ref, sems.at[groups])
    for copy in (*copies, carry):
        copy.start()

    acc_ref[...] = jnp.zeros_like(acc_ref)
    odd = basis_ref[0] % 2
    occ_ref[...] = table_ref[...]
    occ_ref[:, pl.ds(pl.multiple_of((1 - odd) * (halo + here), BB), halo)] = pair_ref[...]
    occ_ref[:, pl.ds(pl.multiple_of(odd * (halo + here), BB), halo)] = next_ref[...]

    def picked(k):
        source = lax.rem(map_ref[0, k, 1] - first + NEAR + blocks, blocks)
        rows = occ_ref[:, pl.ds(pl.multiple_of(source * BB, BB), BB)]
        return jnp.where(k < count_ref[0, 0], rows, jnp.zeros_like(rows))

    for g in range(groups):
        copies[g].wait()
        sums = []
        for j in range(0, per, 2):
            k = g * per + j
            if j + 1 < per:
                one, two = picked(k), picked(k + 1)
                none = jnp.zeros_like(one)
                left = jnp.concatenate(
                    [jnp.concatenate([one, none], axis=1), jnp.concatenate([none, two], axis=1)], axis=0
                )
                right = jnp.concatenate([buf_ref[g, :, j], buf_ref[g, :, j + 1]], axis=-1).reshape(q * BB, 2 * BB)
            else:
                left, right = picked(k), buf_ref[g, :, j].reshape(q * BB, BB)
            sums.append(lax.dot_general(left, right, (((1,), (1,)), ((), ())), preferred_element_type=F32))
        for j in range(per):
            rows = sums[j // 2][(j % 2) * nocc : (j % 2 + 1) * nocc]
            target = pl.multiple_of((map_ref[0, g * per + j, 0] - first) * BB, BB)
            for p in range(q):
                acc_ref[p * nocc : (p + 1) * nocc, pl.ds(target, BB)] += rows[:, p * BB : (p + 1) * BB]
    out_ref[...] = acc_ref[...].astype(BF16)
    carry.wait()


def half_rows(basis, pair_map, pair_count, table, pair, after, v_blocks, virt, blocks, width, following):
    q, pairs = v_blocks.shape[:2]
    nocc, halo = pair.shape
    here = table.shape[1] - 2 * halo
    groups = pairs // divisor(pairs, 4)
    return pl.pallas_call(
        functools.partial(half_kernel, groups, blocks, following),
        in_specs=[SMEM, SMEM, SMEM, VMEM, VMEM, VMEM, HBM, HBM],
        out_specs=[VMEM, VMEM],
        scratch_shapes=[
            pltpu.VMEM((groups, q, pairs // groups, BB, BB), BF16),
            pltpu.VMEM((q * nocc, here), F32),
            pltpu.VMEM((nocc, here + 2 * halo), BF16),
            pltpu.SemaphoreType.DMA((groups + 1,)),
        ],
        out_shape=[
            jax.ShapeDtypeStruct((q * nocc, here), BF16),
            jax.ShapeDtypeStruct((carried(virt.shape[0]), width), BF16),
        ],
        compiler_params=pltpu.CompilerParams(vmem_limit_bytes=50 * 2**20),
        cost_estimate=pl.CostEstimate(
            flops=2 * v_blocks.size * nocc, bytes_accessed=2 * v_blocks.size, transcendentals=0
        ),
    )(basis, pair_map, pair_count, table, pair, after, v_blocks, virt)


def carried(depth):
    return min(768, depth // 2)


def cuts_of(depth):
    start = carried(depth)
    return [(at, min(768, depth - at)) for at in range(start, depth, 768)]


def joined(refs):
    return jnp.concatenate([ref[...] for ref in refs], axis=0).astype(F32)


def product_kernel(step, kept, following, parts, adds, basis_ref, virt_ref, first_ref, *refs):
    half_refs, refs = refs[:parts], refs[parts:]
    add_refs = refs[: sum(adds)]
    out_ref, *carry_refs, buf_ref, acc_ref, sems = refs[-5 if following else -4 :]
    width = acc_ref.shape[1]
    columns = chunk_columns(basis_ref[0], step, kept, width)
    cuts = cuts_of(virt_ref.shape[0])
    copies = [
        pltpu.make_async_copy(
            virt_ref.at[pl.ds(start, size), columns], buf_ref.at[pl.ds(start - cuts[0][0], size)], sems.at[i]
        )
        for i, (start, size) in enumerate(cuts)
    ]
    for carry_ref in carry_refs:
        after = chunk_columns(basis_ref[0], *following, width)
        copies.append(
            pltpu.make_async_copy(
                virt_ref.at[pl.ds(0, carry_ref.shape[0]), after], carry_ref, sems.at[len(cuts)]
            )
        )
    for copy in copies:
        copy.start()

    def term(start, block):
        rows = jnp.concatenate([ref[:, start : start + block.shape[0]] for ref in half_refs], axis=0)
        return jnp.dot(rows, block, preferred_element_type=F32)

    total = term(0, first_ref[...])
    at = 0
    for count in adds:
        total += joined(add_refs[at : at + count])
        at += count
    acc_ref[...] = total
    for i, (start, size) in enumerate(cuts):
        copies[i].wait()
        total = acc_ref[...] + term(start, buf_ref[start - cuts[0][0] : start - cuts[0][0] + size])
        if i < len(cuts) - 1:
            acc_ref[...] = total
        else:
            out_ref[...] = total.astype(out_ref.dtype)
    for copy in copies[len(cuts) :]:
        copy.wait()


def product(basis, virt, first, step, kept, following, parts, adds=(), after=(), dtype=BF16):
    rows = sum(part.shape[0] for part in parts)
    depth, width = virt.shape[0], first.shape[1]
    flat = [block for add in adds for block in add]
    shapes = [jax.ShapeDtypeStruct((rows, width), dtype)]
    if following:
        shapes.append(jax.ShapeDtypeStruct(first.shape, BF16))
    return pl.pallas_call(
        functools.partial(product_kernel, step, kept, following, len(parts), tuple(len(add) for add in adds)),
        in_specs=[SMEM, HBM] + [VMEM] * (1 + len(parts) + len(flat)) + [ANY] * len(after),
        out_specs=[VMEM] * len(shapes),
        scratch_shapes=[
            pltpu.VMEM((depth - first.shape[0], width), BF16),
            pltpu.VMEM((rows, width), F32),
            pltpu.SemaphoreType.DMA((len(cuts_of(depth)) + 1,)),
        ],
        out_shape=shapes,
        compiler_params=pltpu.CompilerParams(vmem_limit_bytes=16 * 2**20),
        cost_estimate=pl.CostEstimate(
            flops=2 * rows * depth * width, bytes_accessed=2 * depth * width, transcendentals=0
        ),
    )(basis, virt, first, *parts, *flat, *after)


def finish_kernel(slab, adds, aux_ref, total_ref, *refs):
    add_refs, (out_ref, acc_ref) = refs[: sum(adds)], refs[-2:]
    total = total_ref[...]
    at = 0
    for count in adds:
        total += joined(add_refs[at : at + count])
        at += count
    acc_ref[...] = total
    for s in range(acc_ref.shape[0] // slab):
        rows = acc_ref[pl.ds(pl.multiple_of((aux_ref[0] ^ s) * slab, slab), slab), :]
        out_ref[:, s * slab : (s + 1) * slab] = rows.T.astype(BF16)


def finish(aux, total, adds, slab):
    flat = [block for add in adds for block in add]
    return pl.pallas_call(
        functools.partial(finish_kernel, slab, tuple(len(add) for add in adds)),
        in_specs=[SMEM] + [VMEM] * (1 + len(flat)),
        out_specs=VMEM,
        scratch_shapes=[pltpu.VMEM(total.shape, F32)],
        out_shape=jax.ShapeDtypeStruct(total.shape[::-1], BF16),
        compiler_params=pltpu.CompilerParams(vmem_limit_bytes=16 * 2**20),
    )(aux, total, *flat)


def local(v_blocks, pair_map, pair_count, occ_coef, virt_coef):
    peers = lax.axis_size("basis")
    slabs = lax.axis_size("aux")
    aux = lax.axis_index("aux").astype(jnp.int32)
    basis = lax.axis_index("basis").astype(jnp.int32)
    blocks = virt_coef.shape[0] // BB * peers
    halo = NEAR * BB

    even = basis % 2 == 0
    first, last = occ_coef[:, :halo], occ_coef[:, -halo:]
    pair = exchange(jnp.where(even, last, first), "basis", 1)
    ring = [(i, (i + 1 if i % 2 else i - 1) % peers) for i in range(peers)]
    after = lax.ppermute(jnp.where(even, first, last), "basis", ring)
    table = jnp.pad(occ_coef, ((0, 0), (halo, halo)))
    width = virt_coef.shape[1] // peers
    groups = peers // 2
    top, second, *others = range(groups - 1, -1, -1)
    sends = [(m, False) for m in (top, second)]
    keeps = [(m, True) for m in (top, second, *others)]
    if groups == 4:
        order = [*sends, *sends, (1, False), keeps[0], keeps[1], keeps[3], (0, False), keeps[2]]
    else:
        order = [*sends, *sends, *((m, False) for m in others), *keeps]
    number = basis.reshape(1)
    own, first = half_rows(
        number, pair_map, pair_count, table, pair, after, v_blocks, virt_coef, blocks, width, order[0]
    )
    carry = [first]

    def mult(step, kept, parts, adds=(), after=(), dtype=BF16):
        assert order.pop(0) == (step, kept)
        following = order[0] if order else None
        out, *carry[:] = product(number, virt_coef, carry[0], step, kept, following, parts, adds, after, dtype)
        return out

    def send(step, parts, after=()):
        return exchange(mult(step, False, parts, after=after), "basis", 1)

    early = [own, exchange(own, "aux", 1)]
    far = [own]
    bit = slabs // 2
    while bit > 1:
        far += [exchange(rows, "aux", bit) for rows in far]
        bit //= 2
    far = far[1:]
    received = {top: (send(top, early),)}
    received[second] = (send(second, early),)
    *far, _, _ = lax.optimization_barrier((*far, carry[0], received[top][0]))
    late = [block for rows in far for block in (rows, exchange(rows, "aux", 1))]
    every = early + late
    received[top] += (send(top, late),)
    received[second] += (send(second, late),)
    if groups == 4:
        received[1] = (send(1, every, received[2][:1]),)
        sent = mult(3, True, every, (received[3],))
        along = lambda pairs: [(2 * a + s, 2 * b + s) for a, b in pairs for s in (0, 1)]
        relayed = lax.ppermute(sent, "basis", along([(0, 1), (3, 2)]))
        inner = lax.ppermute(sent, "basis", along([(1, 2), (2, 1)]))
        part = mult(2, True, every, (received[2],), dtype=F32)
        total = mult(0, True, every, dtype=F32)
        sent = (part + relayed.astype(F32)).astype(BF16)
        third = exchange(sent, "basis", 4)
        received[0] = (send(0, every, after=(sent,)),)
        last = mult(1, True, every, (received[1],), after=(inner,))
        fourth = exchange(last, "basis", 2)
        third, first_kept = lax.optimization_barrier((third, received[0][0]))
        received[0] = (first_kept,)
        adds = (received[0], (inner,), (third,), (fourth,))
    else:
        for m in others:
            received[m] = (send(m, every),)
        adds = (received[0],)
        for m in (top, second, *others[:-1]):
            sent = mult(m, True, every, (received[m],))
            adds += ((exchange(sent, "basis", 2 * m),),)
        total = mult(0, True, every, dtype=F32)
    return finish(aux.reshape(1), total, adds, own.shape[0])


def solution(mesh):
    in_specs = (
        P("aux", "basis", None, None),
        P("aux", "basis", None),
        P("aux", "basis"),
        P(None, "basis"),
        P("basis", "aux"),
    )
    out_specs = P(("aux", "basis"), None)
    return jax.shard_map(local, mesh=mesh, in_specs=in_specs, out_specs=out_specs, check_vma=False)
```

```python
import functools

import jax
import jax.numpy as jnp
from jax import lax
from jax.experimental import pallas as pl
from jax.experimental.pallas import tpu as pltpu
from jax.sharding import PartitionSpec as P

BB = 128
NEAR = 8
F32 = jnp.float32
BF16 = jnp.bfloat16
VMEM = pl.BlockSpec(memory_space=pltpu.VMEM)
SMEM = pl.BlockSpec(memory_space=pltpu.SMEM)
HBM = pl.BlockSpec(memory_space=pltpu.HBM)
ANY = pl.BlockSpec(memory_space=pl.ANY)


def exchange(array, axis, bit):
    peers = lax.axis_size(axis)
    return lax.ppermute(array, axis, [(i, i ^ bit) for i in range(peers)])


def divisor(length, most):
    return max(d for d in range(1, most + 1) if length % d == 0)


def chunk_columns(basis, step, kept, width):
    chunk = basis ^ (2 * step + (0 if kept else 1))
    return pl.ds(pl.multiple_of(chunk * width, BB), width)


def half_kernel(
    groups, blocks, following, basis_ref, map_ref, count_ref, table_ref, pair_ref, next_ref, v_ref, virt_ref,
    out_ref, carry_ref, buf_ref, acc_ref, occ_ref, sems,
):
    q = v_ref.shape[0]
    nocc, halo = pair_ref.shape
    here = table_ref.shape[1] - 2 * halo
    per = v_ref.shape[1] // groups
    blocks_here = here // BB
    first = basis_ref[0] * blocks_here
    copies = [
        pltpu.make_async_copy(v_ref.at[:, pl.ds(g * per, per)], buf_ref.at[g], sems.at[g]) for g in range(groups)
    ]
    columns = chunk_columns(basis_ref[0], *following, carry_ref.shape[1])
    carry = pltpu.make_async_copy(virt_ref.at[pl.ds(0, carry_ref.shape[0]), columns], carry_ref, sems.at[groups])
    for copy in (*copies, carry):
        copy.start()

    acc_ref[...] = jnp.zeros_like(acc_ref)
    odd = basis_ref[0] % 2
    occ_ref[...] = table_ref[...]
    occ_ref[:, pl.ds(pl.multiple_of((1 - odd) * (halo + here), BB), halo)] = pair_ref[...]
    occ_ref[:, pl.ds(pl.multiple_of(odd * (halo + here), BB), halo)] = next_ref[...]

    def picked(k):
        source = lax.rem(map_ref[0, k, 1] - first + NEAR + blocks, blocks)
        rows = occ_ref[:, pl.ds(pl.multiple_of(source * BB, BB), BB)]
        return jnp.where(k < count_ref[0, 0], rows, jnp.zeros_like(rows))

    for g in range(groups):
        copies[g].wait()
        sums = []
        for j in range(0, per, 2):
            k = g * per + j
            if j + 1 < per:
                one, two = picked(k), picked(k + 1)
                none = jnp.zeros_like(one)
                left = jnp.concatenate(
                    [jnp.concatenate([one, none], axis=1), jnp.concatenate([none, two], axis=1)], axis=0
                )
                right = jnp.concatenate([buf_ref[g, :, j], buf_ref[g, :, j + 1]], axis=-1).reshape(q * BB, 2 * BB)
            else:
                left, right = picked(k), buf_ref[g, :, j].reshape(q * BB, BB)
            sums.append(lax.dot_general(left, right, (((1,), (1,)), ((), ())), preferred_element_type=F32))
        for j in range(per):
            rows = sums[j // 2][(j % 2) * nocc : (j % 2 + 1) * nocc]
            target = pl.multiple_of((map_ref[0, g * per + j, 0] - first) * BB, BB)
            for p in range(q):
                acc_ref[p * nocc : (p + 1) * nocc, pl.ds(target, BB)] += rows[:, p * BB : (p + 1) * BB]
    out_ref[...] = acc_ref[...].astype(BF16)
    carry.wait()


def half_rows(basis, pair_map, pair_count, table, pair, after, v_blocks, virt, blocks, width, following):
    q, pairs = v_blocks.shape[:2]
    nocc, halo = pair.shape
    here = table.shape[1] - 2 * halo
    groups = pairs // divisor(pairs, 4)
    return pl.pallas_call(
        functools.partial(half_kernel, groups, blocks, following),
        in_specs=[SMEM, SMEM, SMEM, VMEM, VMEM, VMEM, HBM, HBM],
        out_specs=[VMEM, VMEM],
        scratch_shapes=[
            pltpu.VMEM((groups, q, pairs // groups, BB, BB), BF16),
            pltpu.VMEM((q * nocc, here), F32),
            pltpu.VMEM((nocc, here + 2 * halo), BF16),
            pltpu.SemaphoreType.DMA((groups + 1,)),
        ],
        out_shape=[
            jax.ShapeDtypeStruct((q * nocc, here), BF16),
            jax.ShapeDtypeStruct((carried(virt.shape[0]), width), BF16),
        ],
        compiler_params=pltpu.CompilerParams(vmem_limit_bytes=50 * 2**20),
        cost_estimate=pl.CostEstimate(
            flops=2 * v_blocks.size * nocc, bytes_accessed=2 * v_blocks.size, transcendentals=0
        ),
    )(basis, pair_map, pair_count, table, pair, after, v_blocks, virt)


def carried(depth):
    return min(768, depth // 2)


def cuts_of(depth):
    start = carried(depth)
    return [(at, min(768, depth - at)) for at in range(start, depth, 768)]


def joined(refs):
    return jnp.concatenate([ref[...] for ref in refs], axis=0).astype(F32)


def product_kernel(step, kept, following, parts, adds, basis_ref, virt_ref, first_ref, *refs):
    half_refs, refs = refs[:parts], refs[parts:]
    add_refs = refs[: sum(adds)]
    out_ref, *carry_refs, buf_ref, acc_ref, sems = refs[-5 if following else -4 :]
    width = acc_ref.shape[1]
    columns = chunk_columns(basis_ref[0], step, kept, width)
    cuts = cuts_of(virt_ref.shape[0])
    copies = [
        pltpu.make_async_copy(
            virt_ref.at[pl.ds(start, size), columns], buf_ref.at[pl.ds(start - cuts[0][0], size)], sems.at[i]
        )
        for i, (start, size) in enumerate(cuts)
    ]
    for carry_ref in carry_refs:
        after = chunk_columns(basis_ref[0], *following, width)
        copies.append(
            pltpu.make_async_copy(
                virt_ref.at[pl.ds(0, carry_ref.shape[0]), after], carry_ref, sems.at[len(cuts)]
            )
        )
    for copy in copies:
        copy.start()

    def term(start, block):
        rows = jnp.concatenate([ref[:, start : start + block.shape[0]] for ref in half_refs], axis=0)
        return jnp.dot(rows, block, preferred_element_type=F32)

    total = term(0, first_ref[...])
    at = 0
    for count in adds:
        total += joined(add_refs[at : at + count])
        at += count
    acc_ref[...] = total
    for i, (start, size) in enumerate(cuts):
        copies[i].wait()
        total = acc_ref[...] + term(start, buf_ref[start - cuts[0][0] : start - cuts[0][0] + size])
        if i < len(cuts) - 1:
            acc_ref[...] = total
        else:
            out_ref[...] = total.astype(out_ref.dtype)
    for copy in copies[len(cuts) :]:
        copy.wait()


def product(basis, virt, first, step, kept, following, parts, adds=(), after=(), dtype=BF16):
    rows = sum(part.shape[0] for part in parts)
    depth, width = virt.shape[0], first.shape[1]
    flat = [block for add in adds for block in add]
    shapes = [jax.ShapeDtypeStruct((rows, width), dtype)]
    if following:
        shapes.append(jax.ShapeDtypeStruct(first.shape, BF16))
    return pl.pallas_call(
        functools.partial(product_kernel, step, kept, following, len(parts), tuple(len(add) for add in adds)),
        in_specs=[SMEM, HBM] + [VMEM] * (1 + len(parts) + len(flat)) + [ANY] * len(after),
        out_specs=[VMEM] * len(shapes),
        scratch_shapes=[
            pltpu.VMEM((depth - first.shape[0], width), BF16),
            pltpu.VMEM((rows, width), F32),
            pltpu.SemaphoreType.DMA((len(cuts_of(depth)) + 1,)),
        ],
        out_shape=shapes,
        compiler_params=pltpu.CompilerParams(vmem_limit_bytes=16 * 2**20),
        cost_estimate=pl.CostEstimate(
            flops=2 * rows * depth * width, bytes_accessed=2 * depth * width, transcendentals=0
        ),
    )(basis, virt, first, *parts, *flat, *after)


def finish_kernel(slab, adds, aux_ref, total_ref, *refs):
    add_refs, (out_ref, acc_ref) = refs[: sum(adds)], refs[-2:]
    total = total_ref[...]
    at = 0
    for count in adds:
        total += joined(add_refs[at : at + count])
        at += count
    acc_ref[...] = total
    for s in range(acc_ref.shape[0] // slab):
        rows = acc_ref[pl.ds(pl.multiple_of((aux_ref[0] ^ s) * slab, slab), slab), :]
        out_ref[:, s * slab : (s + 1) * slab] = rows.T.astype(BF16)


def finish(aux, total, adds, slab):
    flat = [block for add in adds for block in add]
    return pl.pallas_call(
        functools.partial(finish_kernel, slab, tuple(len(add) for add in adds)),
        in_specs=[SMEM] + [VMEM] * (1 + len(flat)),
        out_specs=VMEM,
        scratch_shapes=[pltpu.VMEM(total.shape, F32)],
        out_shape=jax.ShapeDtypeStruct(total.shape[::-1], BF16),
        compiler_params=pltpu.CompilerParams(vmem_limit_bytes=16 * 2**20),
    )(aux, total, *flat)


def local(v_blocks, pair_map, pair_count, occ_coef, virt_coef):
    peers = lax.axis_size("basis")
    slabs = lax.axis_size("aux")
    aux = lax.axis_index("aux").astype(jnp.int32)
    basis = lax.axis_index("basis").astype(jnp.int32)
    blocks = virt_coef.shape[0] // BB * peers
    halo = NEAR * BB

    even = basis % 2 == 0
    first, last = occ_coef[:, :halo], occ_coef[:, -halo:]
    pair = exchange(jnp.where(even, last, first), "basis", 1)
    ring = [(i, (i + 1 if i % 2 else i - 1) % peers) for i in range(peers)]
    after = lax.ppermute(jnp.where(even, first, last), "basis", ring)
    table = jnp.pad(occ_coef, ((0, 0), (halo, halo)))
    width = virt_coef.shape[1] // peers
    groups = peers // 2
    top, second, *others = range(groups - 1, -1, -1)
    sends = [(m, False) for m in (top, second)]
    keeps = [(m, True) for m in (top, second, *others)]
    if groups == 4:
        order = [*sends, *sends, (1, False), keeps[0], keeps[1], keeps[3], keeps[2], (0, False)]
    else:
        order = [*sends, *sends, *((m, False) for m in others), *keeps]
    number = basis.reshape(1)
    own, first = half_rows(
        number, pair_map, pair_count, table, pair, after, v_blocks, virt_coef, blocks, width, order[0]
    )
    carry = [first]

    def mult(step, kept, parts, adds=(), after=(), dtype=BF16):
        assert order.pop(0) == (step, kept)
        following = order[0] if order else None
        out, *carry[:] = product(number, virt_coef, carry[0], step, kept, following, parts, adds, after, dtype)
        return out

    def send(step, parts, after=()):
        return exchange(mult(step, False, parts, after=after), "basis", 1)

    early = [own, exchange(own, "aux", 1)]
    far = [own]
    bit = slabs // 2
    while bit > 1:
        far += [exchange(rows, "aux", bit) for rows in far]
        bit //= 2
    far = far[1:]
    received = {top: (send(top, early),)}
    received[second] = (send(second, early),)
    *far, _, _ = lax.optimization_barrier((*far, carry[0], received[top][0]))
    late = [block for rows in far for block in (rows, exchange(rows, "aux", 1))]
    every = early + late
    received[top] += (send(top, late),)
    received[second] += (send(second, late),)
    if groups == 4:
        received[1] = (send(1, every, received[2][:1]),)
        sent = mult(3, True, every, (received[3],))
        along = lambda pairs: [(2 * a + s, 2 * b + s) for a, b in pairs for s in (0, 1)]
        relayed = lax.ppermute(sent, "basis", along([(0, 1), (3, 2)]))
        inner = lax.ppermute(sent, "basis", along([(1, 2), (2, 1)]))
        part = mult(2, True, every, (received[2],), dtype=F32)
        total = mult(0, True, every, dtype=F32)
        last = mult(1, True, every, (received[1],))
        fourth = exchange(last, "basis", 2)
        sent = (part + relayed.astype(F32)).astype(BF16)
        third = exchange(sent, "basis", 4)
        first_kept = send(0, every, after=(sent, inner))
        third, fourth = lax.optimization_barrier((third, fourth))
        received[0] = (first_kept,)
        adds = (received[0], (inner,), (third,), (fourth,))
    else:
        for m in others:
            received[m] = (send(m, every),)
        adds = (received[0],)
        for m in (top, second, *others[:-1]):
            sent = mult(m, True, every, (received[m],))
            adds += ((exchange(sent, "basis", 2 * m),),)
        total = mult(0, True, every, dtype=F32)
    return finish(aux.reshape(1), total, adds, own.shape[0])


def solution(mesh):
    in_specs = (
        P("aux", "basis", None, None),
        P("aux", "basis", None),
        P("aux", "basis"),
        P(None, "basis"),
        P("basis", "aux"),
    )
    out_specs = P(("aux", "basis"), None)
    return jax.shard_map(local, mesh=mesh, in_specs=in_specs, out_specs=out_specs, check_vma=False)
```

```python
import functools

import jax
import jax.numpy as jnp
from jax import lax
from jax.experimental import pallas as pl
from jax.experimental.pallas import tpu as pltpu
from jax.sharding import PartitionSpec as P

BB = 128
NEAR = 8
SECOND, THIRD = -1, -2
F32 = jnp.float32
BF16 = jnp.bfloat16
VMEM = pl.BlockSpec(memory_space=pltpu.VMEM)
SMEM = pl.BlockSpec(memory_space=pltpu.SMEM)
HBM = pl.BlockSpec(memory_space=pltpu.HBM)
ANY = pl.BlockSpec(memory_space=pl.ANY)


def exchange(array, axis, bit):
    peers = lax.axis_size(axis)
    return lax.ppermute(array, axis, [(i, i ^ bit) for i in range(peers)])


def divisor(length, most):
    return max(d for d in range(1, most + 1) if length % d == 0)


def chunk_columns(basis, step, kept, width):
    if step in (SECOND, THIRD):
        inside = ((basis >> 1) ^ (basis >> 2)) & 1
        step = 2 - inside if step == SECOND else 1 + inside
    chunk = basis ^ (2 * step + (0 if kept else 1))
    return pl.ds(pl.multiple_of(chunk * width, BB), width)


def half_kernel(
    groups, blocks, following, basis_ref, map_ref, count_ref, table_ref, pair_ref, next_ref, v_ref, virt_ref,
    out_ref, carry_ref, buf_ref, acc_ref, occ_ref, sems,
):
    q = v_ref.shape[0]
    nocc, halo = pair_ref.shape
    here = table_ref.shape[1] - 2 * halo
    per = v_ref.shape[1] // groups
    blocks_here = here // BB
    first = basis_ref[0] * blocks_here
    copies = [
        pltpu.make_async_copy(v_ref.at[:, pl.ds(g * per, per)], buf_ref.at[g], sems.at[g]) for g in range(groups)
    ]
    columns = chunk_columns(basis_ref[0], *following, carry_ref.shape[1])
    carry = pltpu.make_async_copy(virt_ref.at[pl.ds(0, carry_ref.shape[0]), columns], carry_ref, sems.at[groups])
    for copy in (*copies, carry):
        copy.start()

    acc_ref[...] = jnp.zeros_like(acc_ref)
    odd = basis_ref[0] % 2
    occ_ref[...] = table_ref[...]
    occ_ref[:, pl.ds(pl.multiple_of((1 - odd) * (halo + here), BB), halo)] = pair_ref[...]
    occ_ref[:, pl.ds(pl.multiple_of(odd * (halo + here), BB), halo)] = next_ref[...]

    def picked(k):
        source = lax.rem(map_ref[0, k, 1] - first + NEAR + blocks, blocks)
        rows = occ_ref[:, pl.ds(pl.multiple_of(source * BB, BB), BB)]
        return jnp.where(k < count_ref[0, 0], rows, jnp.zeros_like(rows))

    for g in range(groups):
        copies[g].wait()
        sums = []
        for j in range(0, per, 2):
            k = g * per + j
            if j + 1 < per:
                one, two = picked(k), picked(k + 1)
                none = jnp.zeros_like(one)
                left = jnp.concatenate(
                    [jnp.concatenate([one, none], axis=1), jnp.concatenate([none, two], axis=1)], axis=0
                )
                right = jnp.concatenate([buf_ref[g, :, j], buf_ref[g, :, j + 1]], axis=-1).reshape(q * BB, 2 * BB)
            else:
                left, right = picked(k), buf_ref[g, :, j].reshape(q * BB, BB)
            sums.append(lax.dot_general(left, right, (((1,), (1,)), ((), ())), preferred_element_type=F32))
        for j in range(per):
            rows = sums[j // 2][(j % 2) * nocc : (j % 2 + 1) * nocc]
            target = pl.multiple_of((map_ref[0, g * per + j, 0] - first) * BB, BB)
            for p in range(q):
                acc_ref[p * nocc : (p + 1) * nocc, pl.ds(target, BB)] += rows[:, p * BB : (p + 1) * BB]
    out_ref[...] = acc_ref[...].astype(BF16)
    carry.wait()


def half_rows(basis, pair_map, pair_count, table, pair, after, v_blocks, virt, blocks, width, following):
    q, pairs = v_blocks.shape[:2]
    nocc, halo = pair.shape
    here = table.shape[1] - 2 * halo
    groups = pairs // divisor(pairs, 4)
    return pl.pallas_call(
        functools.partial(half_kernel, groups, blocks, following),
        in_specs=[SMEM, SMEM, SMEM, VMEM, VMEM, VMEM, HBM, HBM],
        out_specs=[VMEM, VMEM],
        scratch_shapes=[
            pltpu.VMEM((groups, q, pairs // groups, BB, BB), BF16),
            pltpu.VMEM((q * nocc, here), F32),
            pltpu.VMEM((nocc, here + 2 * halo), BF16),
            pltpu.SemaphoreType.DMA((groups + 1,)),
        ],
        out_shape=[
            jax.ShapeDtypeStruct((q * nocc, here), BF16),
            jax.ShapeDtypeStruct((carried(virt.shape[0]), width), BF16),
        ],
        compiler_params=pltpu.CompilerParams(vmem_limit_bytes=50 * 2**20),
        cost_estimate=pl.CostEstimate(
            flops=2 * v_blocks.size * nocc, bytes_accessed=2 * v_blocks.size, transcendentals=0
        ),
    )(basis, pair_map, pair_count, table, pair, after, v_blocks, virt)


def carried(depth):
    return min(768, depth // 2)


def cuts_of(depth):
    start = carried(depth)
    return [(at, min(768, depth - at)) for at in range(start, depth, 768)]


def joined(refs):
    return jnp.concatenate([ref[...] for ref in refs], axis=0).astype(F32)


def product_kernel(step, kept, following, parts, adds, basis_ref, virt_ref, first_ref, *refs):
    half_refs, refs = refs[:parts], refs[parts:]
    add_refs = refs[: sum(adds)]
    out_ref, *carry_refs, buf_ref, acc_ref, sems = refs[-5 if following else -4 :]
    width = acc_ref.shape[1]
    columns = chunk_columns(basis_ref[0], step, kept, width)
    cuts = cuts_of(virt_ref.shape[0])
    copies = [
        pltpu.make_async_copy(
            virt_ref.at[pl.ds(start, size), columns], buf_ref.at[pl.ds(start - cuts[0][0], size)], sems.at[i]
        )
        for i, (start, size) in enumerate(cuts)
    ]
    for carry_ref in carry_refs:
        after = chunk_columns(basis_ref[0], *following, width)
        copies.append(
            pltpu.make_async_copy(
                virt_ref.at[pl.ds(0, carry_ref.shape[0]), after], carry_ref, sems.at[len(cuts)]
            )
        )
    for copy in copies:
        copy.start()

    def term(start, block):
        rows = jnp.concatenate([ref[:, start : start + block.shape[0]] for ref in half_refs], axis=0)
        return jnp.dot(rows, block, preferred_element_type=F32)

    total = term(0, first_ref[...])
    at = 0
    for count in adds:
        total += joined(add_refs[at : at + count])
        at += count
    acc_ref[...] = total
    for i, (start, size) in enumerate(cuts):
        copies[i].wait()
        total = acc_ref[...] + term(start, buf_ref[start - cuts[0][0] : start - cuts[0][0] + size])
        if i < len(cuts) - 1:
            acc_ref[...] = total
        else:
            out_ref[...] = total.astype(out_ref.dtype)
    for copy in copies[len(cuts) :]:
        copy.wait()


def product(basis, virt, first, step, kept, following, parts, adds=(), after=(), dtype=BF16):
    rows = sum(part.shape[0] for part in parts)
    depth, width = virt.shape[0], first.shape[1]
    flat = [block for add in adds for block in add]
    shapes = [jax.ShapeDtypeStruct((rows, width), dtype)]
    if following:
        shapes.append(jax.ShapeDtypeStruct(first.shape, BF16))
    return pl.pallas_call(
        functools.partial(product_kernel, step, kept, following, len(parts), tuple(len(add) for add in adds)),
        in_specs=[SMEM, HBM] + [VMEM] * (1 + len(parts) + len(flat)) + [ANY] * len(after),
        out_specs=[VMEM] * len(shapes),
        scratch_shapes=[
            pltpu.VMEM((depth - first.shape[0], width), BF16),
            pltpu.VMEM((rows, width), F32),
            pltpu.SemaphoreType.DMA((len(cuts_of(depth)) + 1,)),
        ],
        out_shape=shapes,
        compiler_params=pltpu.CompilerParams(vmem_limit_bytes=16 * 2**20),
        cost_estimate=pl.CostEstimate(
            flops=2 * rows * depth * width, bytes_accessed=2 * depth * width, transcendentals=0
        ),
    )(basis, virt, first, *parts, *flat, *after)


def finish_kernel(slab, adds, aux_ref, total_ref, *refs):
    add_refs, (out_ref, acc_ref) = refs[: sum(adds)], refs[-2:]
    total = total_ref[...]
    at = 0
    for count in adds:
        total += joined(add_refs[at : at + count])
        at += count
    acc_ref[...] = total
    for s in range(acc_ref.shape[0] // slab):
        rows = acc_ref[pl.ds(pl.multiple_of((aux_ref[0] ^ s) * slab, slab), slab), :]
        out_ref[:, s * slab : (s + 1) * slab] = rows.T.astype(BF16)


def finish(aux, total, adds, slab):
    flat = [block for add in adds for block in add]
    return pl.pallas_call(
        functools.partial(finish_kernel, slab, tuple(len(add) for add in adds)),
        in_specs=[SMEM] + [VMEM] * (1 + len(flat)),
        out_specs=VMEM,
        scratch_shapes=[pltpu.VMEM(total.shape, F32)],
        out_shape=jax.ShapeDtypeStruct(total.shape[::-1], BF16),
        compiler_params=pltpu.CompilerParams(vmem_limit_bytes=16 * 2**20),
    )(aux, total, *flat)


def local(v_blocks, pair_map, pair_count, occ_coef, virt_coef):
    peers = lax.axis_size("basis")
    slabs = lax.axis_size("aux")
    aux = lax.axis_index("aux").astype(jnp.int32)
    basis = lax.axis_index("basis").astype(jnp.int32)
    blocks = virt_coef.shape[0] // BB * peers
    halo = NEAR * BB

    even = basis % 2 == 0
    first, last = occ_coef[:, :halo], occ_coef[:, -halo:]
    pair = exchange(jnp.where(even, last, first), "basis", 1)
    ring = [(i, (i + 1 if i % 2 else i - 1) % peers) for i in range(peers)]
    after = lax.ppermute(jnp.where(even, first, last), "basis", ring)
    table = jnp.pad(occ_coef, ((0, 0), (halo, halo)))
    width = virt_coef.shape[1] // peers
    groups = peers // 2
    top, second, *others = range(groups - 1, -1, -1)
    if groups == 4:
        second, others = SECOND, [THIRD, 0]
    sends = [(m, False) for m in (top, second)]
    keeps = [(m, True) for m in (top, second, *others)]
    if groups == 4:
        order = [*sends, *sends, (THIRD, False), *keeps[:2], keeps[3], keeps[2], (0, False)]
    else:
        order = [*sends, *sends, *((m, False) for m in others), *keeps]
    number = basis.reshape(1)
    own, first = half_rows(
        number, pair_map, pair_count, table, pair, after, v_blocks, virt_coef, blocks, width, order[0]
    )
    carry = [first]

    def mult(step, kept, parts, adds=(), after=(), dtype=BF16):
        assert order.pop(0) == (step, kept)
        following = order[0] if order else None
        out, *carry[:] = product(number, virt_coef, carry[0], step, kept, following, parts, adds, after, dtype)
        return out

    def send(step, parts, after=()):
        return exchange(mult(step, False, parts, after=after), "basis", 1)

    early = [own, exchange(own, "aux", 1)]
    far = [own]
    bit = slabs // 2
    while bit > 1:
        far += [exchange(rows, "aux", bit) for rows in far]
        bit //= 2
    far = far[1:]
    received = {top: (send(top, early),)}
    received[second] = (send(second, early),)
    *far, _, _ = lax.optimization_barrier((*far, carry[0], received[top][0]))
    late = [block for rows in far for block in (rows, exchange(rows, "aux", 1))]
    every = early + late
    received[top] += (send(top, late),)
    received[second] += (send(second, late),)
    if groups == 4:
        received[THIRD] = (send(THIRD, every, received[SECOND][:1]),)
        sent = mult(3, True, every, (received[3],))
        along = lambda pairs: [(2 * a + s, 2 * b + s) for a, b in pairs for s in (0, 1)]
        relayed = lax.ppermute(sent, "basis", along([(0, 1), (3, 2)]))
        inner = lax.ppermute(sent, "basis", along([(1, 2), (2, 1)]))
        sent = mult(SECOND, True, every, (received[SECOND],))
        third = lax.ppermute(sent, "basis", along([(0, 2), (3, 1), (1, 0), (2, 3)]))
        total = mult(0, True, every, dtype=F32)
        part = mult(THIRD, True, every, (received[THIRD],), dtype=F32)
        sent = (part + relayed.astype(F32)).astype(BF16)
        fourth = lax.ppermute(sent, "basis", along([(1, 3), (2, 0), (0, 1), (3, 2)]))
        received[0] = (send(0, every, after=(sent, inner)),)
        third, fourth = lax.optimization_barrier((third, fourth))
        adds = (received[0], (inner,), (third,), (fourth,))
    else:
        for m in others:
            received[m] = (send(m, every),)
        adds = (received[0],)
        for m in (top, second, *others[:-1]):
            sent = mult(m, True, every, (received[m],))
            adds += ((exchange(sent, "basis", 2 * m),),)
        total = mult(0, True, every, dtype=F32)
    return finish(aux.reshape(1), total, adds, own.shape[0])


def solution(mesh):
    in_specs = (
        P("aux", "basis", None, None),
        P("aux", "basis", None),
        P("aux", "basis"),
        P(None, "basis"),
        P("basis", "aux"),
    )
    out_specs = P(("aux", "basis"), None)
    return jax.shard_map(local, mesh=mesh, in_specs=in_specs, out_specs=out_specs, check_vma=False)
```

```python
import functools

import jax
import jax.numpy as jnp
from jax import lax
from jax.experimental import pallas as pl
from jax.experimental.pallas import tpu as pltpu
from jax.sharding import PartitionSpec as P

BB = 128
NEAR = 8
SECOND, THIRD = -1, -2
F32 = jnp.float32
BF16 = jnp.bfloat16
VMEM = pl.BlockSpec(memory_space=pltpu.VMEM)
SMEM = pl.BlockSpec(memory_space=pltpu.SMEM)
HBM = pl.BlockSpec(memory_space=pltpu.HBM)
ANY = pl.BlockSpec(memory_space=pl.ANY)


def exchange(array, axis, bit):
    peers = lax.axis_size(axis)
    return lax.ppermute(array, axis, [(i, i ^ bit) for i in range(peers)])


def divisor(length, most):
    return max(d for d in range(1, most + 1) if length % d == 0)


def chunk_columns(basis, step, kept, width):
    if step in (SECOND, THIRD):
        inside = ((basis >> 1) ^ (basis >> 2)) & 1
        step = 2 - inside if step == SECOND else 1 + inside
    chunk = basis ^ (2 * step + (0 if kept else 1))
    return pl.ds(pl.multiple_of(chunk * width, BB), width)


def half_kernel(
    groups, blocks, following, basis_ref, map_ref, count_ref, table_ref, pair_ref, next_ref, v_ref, virt_ref,
    out_ref, carry_ref, buf_ref, acc_ref, occ_ref, sems,
):
    q = v_ref.shape[0]
    nocc, halo = pair_ref.shape
    here = table_ref.shape[1] - 2 * halo
    per = v_ref.shape[1] // groups
    blocks_here = here // BB
    first = basis_ref[0] * blocks_here
    copies = [
        pltpu.make_async_copy(v_ref.at[:, pl.ds(g * per, per)], buf_ref.at[g], sems.at[g]) for g in range(groups)
    ]
    columns = chunk_columns(basis_ref[0], *following, carry_ref.shape[1])
    carry = pltpu.make_async_copy(virt_ref.at[pl.ds(0, carry_ref.shape[0]), columns], carry_ref, sems.at[groups])
    for copy in (*copies, carry):
        copy.start()

    acc_ref[...] = jnp.zeros_like(acc_ref)
    odd = basis_ref[0] % 2
    occ_ref[...] = table_ref[...]
    occ_ref[:, pl.ds(pl.multiple_of((1 - odd) * (halo + here), BB), halo)] = pair_ref[...]
    occ_ref[:, pl.ds(pl.multiple_of(odd * (halo + here), BB), halo)] = next_ref[...]

    def picked(k):
        source = lax.rem(map_ref[0, k, 1] - first + NEAR + blocks, blocks)
        rows = occ_ref[:, pl.ds(pl.multiple_of(source * BB, BB), BB)]
        return jnp.where(k < count_ref[0, 0], rows, jnp.zeros_like(rows))

    for g in range(groups):
        copies[g].wait()
        sums = []
        for j in range(0, per, 2):
            k = g * per + j
            if j + 1 < per:
                one, two = picked(k), picked(k + 1)
                none = jnp.zeros_like(one)
                left = jnp.concatenate(
                    [jnp.concatenate([one, none], axis=1), jnp.concatenate([none, two], axis=1)], axis=0
                )
                right = jnp.concatenate([buf_ref[g, :, j], buf_ref[g, :, j + 1]], axis=-1).reshape(q * BB, 2 * BB)
            else:
                left, right = picked(k), buf_ref[g, :, j].reshape(q * BB, BB)
            sums.append(lax.dot_general(left, right, (((1,), (1,)), ((), ())), preferred_element_type=F32))
        for j in range(per):
            rows = sums[j // 2][(j % 2) * nocc : (j % 2 + 1) * nocc]
            target = pl.multiple_of((map_ref[0, g * per + j, 0] - first) * BB, BB)
            for p in range(q):
                acc_ref[p * nocc : (p + 1) * nocc, pl.ds(target, BB)] += rows[:, p * BB : (p + 1) * BB]
    out_ref[...] = acc_ref[...].astype(BF16)
    carry.wait()


def half_rows(basis, pair_map, pair_count, table, pair, after, v_blocks, virt, blocks, width, following):
    q, pairs = v_blocks.shape[:2]
    nocc, halo = pair.shape
    here = table.shape[1] - 2 * halo
    groups = pairs // divisor(pairs, 4)
    return pl.pallas_call(
        functools.partial(half_kernel, groups, blocks, following),
        in_specs=[SMEM, SMEM, SMEM, VMEM, VMEM, VMEM, HBM, HBM],
        out_specs=[VMEM, VMEM],
        scratch_shapes=[
            pltpu.VMEM((groups, q, pairs // groups, BB, BB), BF16),
            pltpu.VMEM((q * nocc, here), F32),
            pltpu.VMEM((nocc, here + 2 * halo), BF16),
            pltpu.SemaphoreType.DMA((groups + 1,)),
        ],
        out_shape=[
            jax.ShapeDtypeStruct((q * nocc, here), BF16),
            jax.ShapeDtypeStruct((carried(virt.shape[0]), width), BF16),
        ],
        compiler_params=pltpu.CompilerParams(vmem_limit_bytes=50 * 2**20),
        cost_estimate=pl.CostEstimate(
            flops=2 * v_blocks.size * nocc, bytes_accessed=2 * v_blocks.size, transcendentals=0
        ),
    )(basis, pair_map, pair_count, table, pair, after, v_blocks, virt)


def carried(depth):
    return min(768, depth // 2)


def cuts_of(depth):
    start = carried(depth)
    return [(at, min(768, depth - at)) for at in range(start, depth, 768)]


def joined(refs):
    return jnp.concatenate([ref[...] for ref in refs], axis=0).astype(F32)


def product_kernel(step, kept, following, parts, adds, basis_ref, virt_ref, first_ref, *refs):
    half_refs, refs = refs[:parts], refs[parts:]
    add_refs = refs[: sum(adds)]
    out_ref, *carry_refs, buf_ref, acc_ref, sems = refs[-5 if following else -4 :]
    width = acc_ref.shape[1]
    columns = chunk_columns(basis_ref[0], step, kept, width)
    cuts = cuts_of(virt_ref.shape[0])
    copies = [
        pltpu.make_async_copy(
            virt_ref.at[pl.ds(start, size), columns], buf_ref.at[pl.ds(start - cuts[0][0], size)], sems.at[i]
        )
        for i, (start, size) in enumerate(cuts)
    ]
    for carry_ref in carry_refs:
        after = chunk_columns(basis_ref[0], *following, width)
        copies.append(
            pltpu.make_async_copy(
                virt_ref.at[pl.ds(0, carry_ref.shape[0]), after], carry_ref, sems.at[len(cuts)]
            )
        )
    for copy in copies:
        copy.start()

    def term(start, block):
        rows = jnp.concatenate([ref[:, start : start + block.shape[0]] for ref in half_refs], axis=0)
        return jnp.dot(rows, block, preferred_element_type=F32)

    total = term(0, first_ref[...])
    at = 0
    for count in adds:
        total += joined(add_refs[at : at + count])
        at += count
    acc_ref[...] = total
    for i, (start, size) in enumerate(cuts):
        copies[i].wait()
        total = acc_ref[...] + term(start, buf_ref[start - cuts[0][0] : start - cuts[0][0] + size])
        if i < len(cuts) - 1:
            acc_ref[...] = total
        else:
            out_ref[...] = total.astype(out_ref.dtype)
    for copy in copies[len(cuts) :]:
        copy.wait()


def product(basis, virt, first, step, kept, following, parts, adds=(), after=(), dtype=BF16):
    rows = sum(part.shape[0] for part in parts)
    depth, width = virt.shape[0], first.shape[1]
    flat = [block for add in adds for block in add]
    shapes = [jax.ShapeDtypeStruct((rows, width), dtype)]
    if following:
        shapes.append(jax.ShapeDtypeStruct(first.shape, BF16))
    return pl.pallas_call(
        functools.partial(product_kernel, step, kept, following, len(parts), tuple(len(add) for add in adds)),
        in_specs=[SMEM, HBM] + [VMEM] * (1 + len(parts) + len(flat)) + [ANY] * len(after),
        out_specs=[VMEM] * len(shapes),
        scratch_shapes=[
            pltpu.VMEM((depth - first.shape[0], width), BF16),
            pltpu.VMEM((rows, width), F32),
            pltpu.SemaphoreType.DMA((len(cuts_of(depth)) + 1,)),
        ],
        out_shape=shapes,
        compiler_params=pltpu.CompilerParams(vmem_limit_bytes=16 * 2**20),
        cost_estimate=pl.CostEstimate(
            flops=2 * rows * depth * width, bytes_accessed=2 * depth * width, transcendentals=0
        ),
    )(basis, virt, first, *parts, *flat, *after)


def finish_kernel(slab, adds, aux_ref, total_ref, *refs):
    add_refs, (out_ref, acc_ref) = refs[: sum(adds)], refs[-2:]
    total = total_ref[...]
    at = 0
    for count in adds:
        total += joined(add_refs[at : at + count])
        at += count
    acc_ref[...] = total
    ordered = [
        acc_ref[pl.ds(pl.multiple_of((aux_ref[0] ^ s) * slab, slab), slab), :]
        for s in range(acc_ref.shape[0] // slab)
    ]
    out_ref[...] = jnp.concatenate(ordered, axis=0).T.astype(BF16)


def finish(aux, total, adds, slab):
    flat = [block for add in adds for block in add]
    return pl.pallas_call(
        functools.partial(finish_kernel, slab, tuple(len(add) for add in adds)),
        in_specs=[SMEM] + [VMEM] * (1 + len(flat)),
        out_specs=VMEM,
        scratch_shapes=[pltpu.VMEM(total.shape, F32)],
        out_shape=jax.ShapeDtypeStruct(total.shape[::-1], BF16),
        compiler_params=pltpu.CompilerParams(vmem_limit_bytes=16 * 2**20),
    )(aux, total, *flat)


def local(v_blocks, pair_map, pair_count, occ_coef, virt_coef):
    peers = lax.axis_size("basis")
    slabs = lax.axis_size("aux")
    aux = lax.axis_index("aux").astype(jnp.int32)
    basis = lax.axis_index("basis").astype(jnp.int32)
    blocks = virt_coef.shape[0] // BB * peers
    halo = NEAR * BB

    even = basis % 2 == 0
    first, last = occ_coef[:, :halo], occ_coef[:, -halo:]
    pair = exchange(jnp.where(even, last, first), "basis", 1)
    ring = [(i, (i + 1 if i % 2 else i - 1) % peers) for i in range(peers)]
    after = lax.ppermute(jnp.where(even, first, last), "basis", ring)
    table = jnp.pad(occ_coef, ((0, 0), (halo, halo)))
    width = virt_coef.shape[1] // peers
    groups = peers // 2
    top, second, *others = range(groups - 1, -1, -1)
    if groups == 4:
        second, others = SECOND, [THIRD, 0]
    sends = [(m, False) for m in (top, second)]
    keeps = [(m, True) for m in (top, second, *others)]
    if groups == 4:
        order = [sends[0], (THIRD, False), *sends, keeps[0], (THIRD, False), keeps[1], keeps[3], keeps[2], (0, False)]
    else:
        order = [sends[0], *sends, *((m, False) for m in others), *keeps]
    number = basis.reshape(1)
    own, first = half_rows(
        number, pair_map, pair_count, table, pair, after, v_blocks, virt_coef, blocks, width, order[0]
    )
    carry = [first]

    def mult(step, kept, parts, adds=(), after=(), dtype=BF16):
        assert order.pop(0) == (step, kept)
        following = order[0] if order else None
        out, *carry[:] = product(number, virt_coef, carry[0], step, kept, following, parts, adds, after, dtype)
        return out

    def send(step, parts, after=()):
        return exchange(mult(step, False, parts, after=after), "basis", 1)

    early = [own, exchange(own, "aux", 1)]
    far = [own]
    bit = slabs // 2
    while bit > 1:
        far += [exchange(rows, "aux", bit) for rows in far]
        bit //= 2
    far = far[1:]
    received = {top: (send(top, early),)}
    if groups == 4:
        received[THIRD] = (send(THIRD, early),)
    *far, _, _ = lax.optimization_barrier((*far, carry[0], received[top][0]))
    late = [block for rows in far for block in (rows, exchange(rows, "aux", 1))]
    every = early + late
    received[top] += (send(top, late),)
    received[second] = (send(second, every, after=received.get(THIRD, ())),)
    if groups == 4:
        sent = mult(3, True, every, (received[3],))
        along = lambda pairs: [(2 * a + s, 2 * b + s) for a, b in pairs for s in (0, 1)]
        relayed = lax.ppermute(sent, "basis", along([(0, 1), (3, 2)]))
        inner = lax.ppermute(sent, "basis", along([(1, 2), (2, 1)]))
        received[THIRD] += (send(THIRD, late),)
        sent = mult(SECOND, True, every, (received[SECOND],))
        third = lax.ppermute(sent, "basis", along([(0, 2), (3, 1), (1, 0), (2, 3)]))
        total = mult(0, True, every, dtype=F32)
        part = mult(THIRD, True, every, (received[THIRD],), dtype=F32)
        sent = (part + relayed.astype(F32)).astype(BF16)
        fourth = lax.ppermute(sent, "basis", along([(1, 3), (2, 0), (0, 1), (3, 2)]))
        received[0] = (send(0, every, after=(sent, inner)),)
        total = total + inner.astype(F32) + third.astype(F32)
        total, fourth = lax.optimization_barrier((total, fourth))
        adds = (received[0], (fourth,))
    else:
        for m in others:
            received[m] = (send(m, every),)
        adds = (received[0],)
        for m in (top, second, *others[:-1]):
            sent = mult(m, True, every, (received[m],))
            adds += ((exchange(sent, "basis", 2 * m),),)
        total = mult(0, True, every, dtype=F32)
    return finish(aux.reshape(1), total, adds, own.shape[0])


def solution(mesh):
    in_specs = (
        P("aux", "basis", None, None),
        P("aux", "basis", None),
        P("aux", "basis"),
        P(None, "basis"),
        P("basis", "aux"),
    )
    out_specs = P(("aux", "basis"), None)
    return jax.shard_map(local, mesh=mesh, in_specs=in_specs, out_specs=out_specs, check_vma=False)
```

```python
import functools

import jax
import jax.numpy as jnp
from jax import lax
from jax.experimental import pallas as pl
from jax.experimental.pallas import tpu as pltpu
from jax.sharding import PartitionSpec as P

BB = 128
NEAR = 8
SECOND, THIRD = -1, -2
F32 = jnp.float32
BF16 = jnp.bfloat16
VMEM = pl.BlockSpec(memory_space=pltpu.VMEM)
SMEM = pl.BlockSpec(memory_space=pltpu.SMEM)
HBM = pl.BlockSpec(memory_space=pltpu.HBM)
ANY = pl.BlockSpec(memory_space=pl.ANY)


def exchange(array, axis, bit):
    peers = lax.axis_size(axis)
    return lax.ppermute(array, axis, [(i, i ^ bit) for i in range(peers)])


def divisor(length, most):
    return max(d for d in range(1, most + 1) if length % d == 0)


def chunk_columns(basis, step, kept, width):
    if step in (SECOND, THIRD):
        inside = ((basis >> 1) ^ (basis >> 2)) & 1
        step = 2 - inside if step == SECOND else 1 + inside
    chunk = basis ^ (2 * step + (0 if kept else 1))
    return pl.ds(pl.multiple_of(chunk * width, BB), width)


def half_kernel(
    groups, blocks, following, basis_ref, map_ref, count_ref, table_ref, pair_ref, next_ref, v_ref, virt_ref,
    out_ref, carry_ref, buf_ref, acc_ref, occ_ref, sems,
):
    q = v_ref.shape[0]
    nocc, halo = pair_ref.shape
    here = table_ref.shape[1] - 2 * halo
    per = v_ref.shape[1] // groups
    blocks_here = here // BB
    first = basis_ref[0] * blocks_here
    copies = [
        pltpu.make_async_copy(v_ref.at[:, pl.ds(g * per, per)], buf_ref.at[g], sems.at[g]) for g in range(groups)
    ]
    columns = chunk_columns(basis_ref[0], *following, carry_ref.shape[1])
    carry = pltpu.make_async_copy(virt_ref.at[pl.ds(0, carry_ref.shape[0]), columns], carry_ref, sems.at[groups])
    for copy in (*copies, carry):
        copy.start()

    acc_ref[...] = jnp.zeros_like(acc_ref)
    odd = basis_ref[0] % 2
    occ_ref[...] = table_ref[...]
    occ_ref[:, pl.ds(pl.multiple_of((1 - odd) * (halo + here), BB), halo)] = pair_ref[...]
    occ_ref[:, pl.ds(pl.multiple_of(odd * (halo + here), BB), halo)] = next_ref[...]

    def picked(k):
        source = lax.rem(map_ref[0, k, 1] - first + NEAR + blocks, blocks)
        rows = occ_ref[:, pl.ds(pl.multiple_of(source * BB, BB), BB)]
        return jnp.where(k < count_ref[0, 0], rows, jnp.zeros_like(rows))

    for g in range(groups):
        copies[g].wait()
        sums = []
        for j in range(0, per, 2):
            k = g * per + j
            if j + 1 < per:
                one, two = picked(k), picked(k + 1)
                none = jnp.zeros_like(one)
                left = jnp.concatenate(
                    [jnp.concatenate([one, none], axis=1), jnp.concatenate([none, two], axis=1)], axis=0
                )
                right = jnp.concatenate([buf_ref[g, :, j], buf_ref[g, :, j + 1]], axis=-1).reshape(q * BB, 2 * BB)
            else:
                left, right = picked(k), buf_ref[g, :, j].reshape(q * BB, BB)
            sums.append(lax.dot_general(left, right, (((1,), (1,)), ((), ())), preferred_element_type=F32))
        for j in range(per):
            rows = sums[j // 2][(j % 2) * nocc : (j % 2 + 1) * nocc]
            target = pl.multiple_of((map_ref[0, g * per + j, 0] - first) * BB, BB)
            for p in range(q):
                acc_ref[p * nocc : (p + 1) * nocc, pl.ds(target, BB)] += rows[:, p * BB : (p + 1) * BB]
    out_ref[...] = acc_ref[...].astype(BF16)
    carry.wait()


def half_rows(basis, pair_map, pair_count, table, pair, after, v_blocks, virt, blocks, width, following):
    q, pairs = v_blocks.shape[:2]
    nocc, halo = pair.shape
    here = table.shape[1] - 2 * halo
    groups = pairs // divisor(pairs, 4)
    return pl.pallas_call(
        functools.partial(half_kernel, groups, blocks, following),
        in_specs=[SMEM, SMEM, SMEM, VMEM, VMEM, VMEM, HBM, HBM],
        out_specs=[VMEM, VMEM],
        scratch_shapes=[
            pltpu.VMEM((groups, q, pairs // groups, BB, BB), BF16),
            pltpu.VMEM((q * nocc, here), F32),
            pltpu.VMEM((nocc, here + 2 * halo), BF16),
            pltpu.SemaphoreType.DMA((groups + 1,)),
        ],
        out_shape=[
            jax.ShapeDtypeStruct((q * nocc, here), BF16),
            jax.ShapeDtypeStruct((carried(virt.shape[0]), width), BF16),
        ],
        compiler_params=pltpu.CompilerParams(vmem_limit_bytes=50 * 2**20),
        cost_estimate=pl.CostEstimate(
            flops=2 * v_blocks.size * nocc, bytes_accessed=2 * v_blocks.size, transcendentals=0
        ),
    )(basis, pair_map, pair_count, table, pair, after, v_blocks, virt)


def carried(depth):
    return min(768, depth // 2)


def cuts_of(depth):
    start = carried(depth)
    return [(at, min(768, depth - at)) for at in range(start, depth, 768)]


def joined(refs):
    return jnp.concatenate([ref[...] for ref in refs], axis=0).astype(F32)


def product_kernel(step, kept, following, parts, adds, basis_ref, virt_ref, first_ref, *refs):
    half_refs, refs = refs[:parts], refs[parts:]
    add_refs = refs[: sum(adds)]
    out_ref, *carry_refs, buf_ref, acc_ref, sems = refs[-5 if following else -4 :]
    width = acc_ref.shape[1]
    columns = chunk_columns(basis_ref[0], step, kept, width)
    cuts = cuts_of(virt_ref.shape[0])
    copies = [
        pltpu.make_async_copy(
            virt_ref.at[pl.ds(start, size), columns], buf_ref.at[pl.ds(start - cuts[0][0], size)], sems.at[i]
        )
        for i, (start, size) in enumerate(cuts)
    ]
    for carry_ref in carry_refs:
        after = chunk_columns(basis_ref[0], *following, width)
        copies.append(
            pltpu.make_async_copy(
                virt_ref.at[pl.ds(0, carry_ref.shape[0]), after], carry_ref, sems.at[len(cuts)]
            )
        )
    for copy in copies:
        copy.start()

    def term(start, block):
        rows = jnp.concatenate([ref[:, start : start + block.shape[0]] for ref in half_refs], axis=0)
        return jnp.dot(rows, block, preferred_element_type=F32)

    total = term(0, first_ref[...])
    at = 0
    for count in adds:
        total += joined(add_refs[at : at + count])
        at += count
    acc_ref[...] = total
    for i, (start, size) in enumerate(cuts):
        copies[i].wait()
        total = acc_ref[...] + term(start, buf_ref[start - cuts[0][0] : start - cuts[0][0] + size])
        if i < len(cuts) - 1:
            acc_ref[...] = total
        else:
            out_ref[...] = total.astype(out_ref.dtype)
    for copy in copies[len(cuts) :]:
        copy.wait()


def product(basis, virt, first, step, kept, following, parts, adds=(), after=(), dtype=BF16):
    rows = sum(part.shape[0] for part in parts)
    depth, width = virt.shape[0], first.shape[1]
    flat = [block for add in adds for block in add]
    shapes = [jax.ShapeDtypeStruct((rows, width), dtype)]
    if following:
        shapes.append(jax.ShapeDtypeStruct(first.shape, BF16))
    return pl.pallas_call(
        functools.partial(product_kernel, step, kept, following, len(parts), tuple(len(add) for add in adds)),
        in_specs=[SMEM, HBM] + [VMEM] * (1 + len(parts) + len(flat)) + [ANY] * len(after),
        out_specs=[VMEM] * len(shapes),
        scratch_shapes=[
            pltpu.VMEM((depth - first.shape[0], width), BF16),
            pltpu.VMEM((rows, width), F32),
            pltpu.SemaphoreType.DMA((len(cuts_of(depth)) + 1,)),
        ],
        out_shape=shapes,
        compiler_params=pltpu.CompilerParams(vmem_limit_bytes=16 * 2**20),
        cost_estimate=pl.CostEstimate(
            flops=2 * rows * depth * width, bytes_accessed=2 * depth * width, transcendentals=0
        ),
    )(basis, virt, first, *parts, *flat, *after)


def finish_kernel(slab, adds, aux_ref, total_ref, *refs):
    add_refs, (out_ref, acc_ref) = refs[: sum(adds)], refs[-2:]
    total = total_ref[...]
    at = 0
    for count in adds:
        total += joined(add_refs[at : at + count])
        at += count
    acc_ref[...] = total
    ordered = [
        acc_ref[pl.ds(pl.multiple_of((aux_ref[0] ^ s) * slab, slab), slab), :]
        for s in range(acc_ref.shape[0] // slab)
    ]
    out_ref[...] = jnp.concatenate(ordered, axis=0).T.astype(BF16)


def finish(aux, total, adds, slab):
    flat = [block for add in adds for block in add]
    return pl.pallas_call(
        functools.partial(finish_kernel, slab, tuple(len(add) for add in adds)),
        in_specs=[SMEM] + [VMEM] * (1 + len(flat)),
        out_specs=VMEM,
        scratch_shapes=[pltpu.VMEM(total.shape, F32)],
        out_shape=jax.ShapeDtypeStruct(total.shape[::-1], BF16),
        compiler_params=pltpu.CompilerParams(vmem_limit_bytes=16 * 2**20),
    )(aux, total, *flat)


def local(v_blocks, pair_map, pair_count, occ_coef, virt_coef):
    peers = lax.axis_size("basis")
    slabs = lax.axis_size("aux")
    aux = lax.axis_index("aux").astype(jnp.int32)
    basis = lax.axis_index("basis").astype(jnp.int32)
    blocks = virt_coef.shape[0] // BB * peers
    halo = NEAR * BB

    even = basis % 2 == 0
    first, last = occ_coef[:, :halo], occ_coef[:, -halo:]
    pair = exchange(jnp.where(even, last, first), "basis", 1)
    ring = [(i, (i + 1 if i % 2 else i - 1) % peers) for i in range(peers)]
    after = lax.ppermute(jnp.where(even, first, last), "basis", ring)
    table = jnp.pad(occ_coef, ((0, 0), (halo, halo)))
    width = virt_coef.shape[1] // peers
    groups = peers // 2
    top, second, *others = range(groups - 1, -1, -1)
    if groups == 4:
        second, others = SECOND, [THIRD, 0]
    sends = [(m, False) for m in (top, second)]
    keeps = [(m, True) for m in (top, second, *others)]
    if groups == 4:
        order = [sends[0], (THIRD, False), *sends, keeps[0], (THIRD, False), *keeps[1:3], (0, False), keeps[3]]
    else:
        order = [sends[0], *sends, *((m, False) for m in others), *keeps]
    number = basis.reshape(1)
    own, first = half_rows(
        number, pair_map, pair_count, table, pair, after, v_blocks, virt_coef, blocks, width, order[0]
    )
    carry = [first]

    def mult(step, kept, parts, adds=(), after=(), dtype=BF16):
        assert order.pop(0) == (step, kept)
        following = order[0] if order else None
        out, *carry[:] = product(number, virt_coef, carry[0], step, kept, following, parts, adds, after, dtype)
        return out

    def send(step, parts, after=()):
        return exchange(mult(step, False, parts, after=after), "basis", 1)

    early = [own, exchange(own, "aux", 1)]
    far = [own]
    bit = slabs // 2
    while bit > 1:
        far += [exchange(rows, "aux", bit) for rows in far]
        bit //= 2
    far = far[1:]
    received = {top: (send(top, early),)}
    if groups == 4:
        received[THIRD] = (send(THIRD, early),)
    *far, _, _ = lax.optimization_barrier((*far, carry[0], received[top][0]))
    late = [block for rows in far for block in (rows, exchange(rows, "aux", 1))]
    every = early + late
    received[top] += (send(top, late),)
    received[second] = (send(second, every, after=received.get(THIRD, ())),)
    if groups == 4:
        sent = mult(3, True, every, (received[3],))
        along = lambda pairs: [(2 * a + s, 2 * b + s) for a, b in pairs for s in (0, 1)]
        relayed = lax.ppermute(sent, "basis", along([(0, 1), (3, 2)]))
        inner = lax.ppermute(sent, "basis", along([(1, 2), (2, 1)]))
        received[THIRD] += (send(THIRD, late),)
        sent = mult(SECOND, True, every, (received[SECOND],))
        third = lax.ppermute(sent, "basis", along([(0, 2), (3, 1), (1, 0), (2, 3)]))
        part = mult(THIRD, True, every, (received[THIRD],), after=(inner,), dtype=F32)
        sent = (part + relayed.astype(F32)).astype(BF16)
        fourth = lax.ppermute(sent, "basis", along([(1, 3), (2, 0), (0, 1), (3, 2)]))
        received[0] = (send(0, every, after=(sent,)),)
        total = mult(0, True, every, dtype=F32)
        total = total + inner.astype(F32) + third.astype(F32)
        total, fourth = lax.optimization_barrier((total, fourth))
        adds = (received[0], (fourth,))
    else:
        for m in others:
            received[m] = (send(m, every),)
        adds = (received[0],)
        for m in (top, second, *others[:-1]):
            sent = mult(m, True, every, (received[m],))
            adds += ((exchange(sent, "basis", 2 * m),),)
        total = mult(0, True, every, dtype=F32)
    return finish(aux.reshape(1), total, adds, own.shape[0])


def solution(mesh):
    in_specs = (
        P("aux", "basis", None, None),
        P("aux", "basis", None),
        P("aux", "basis"),
        P(None, "basis"),
        P("basis", "aux"),
    )
    out_specs = P(("aux", "basis"), None)
    return jax.shard_map(local, mesh=mesh, in_specs=in_specs, out_specs=out_specs, check_vma=False)
```

```python
import functools

import jax
import jax.numpy as jnp
from jax import lax
from jax.experimental import pallas as pl
from jax.experimental.pallas import tpu as pltpu
from jax.sharding import PartitionSpec as P

BB = 128
NEAR = 8
SECOND, THIRD = -1, -2
F32 = jnp.float32
BF16 = jnp.bfloat16
VMEM = pl.BlockSpec(memory_space=pltpu.VMEM)
SMEM = pl.BlockSpec(memory_space=pltpu.SMEM)
HBM = pl.BlockSpec(memory_space=pltpu.HBM)
ANY = pl.BlockSpec(memory_space=pl.ANY)


def exchange(array, axis, bit):
    peers = lax.axis_size(axis)
    return lax.ppermute(array, axis, [(i, i ^ bit) for i in range(peers)])


def divisor(length, most):
    return max(d for d in range(1, most + 1) if length % d == 0)


def chunk_columns(basis, step, kept, width):
    if step in (SECOND, THIRD):
        inside = ((basis >> 1) ^ (basis >> 2)) & 1
        step = 2 - inside if step == SECOND else 1 + inside
    chunk = basis ^ (2 * step + (0 if kept else 1))
    return pl.ds(pl.multiple_of(chunk * width, BB), width)


def half_kernel(
    groups, blocks, following, basis_ref, map_ref, count_ref, table_ref, pair_ref, next_ref, v_ref, virt_ref,
    out_ref, carry_ref, buf_ref, acc_ref, occ_ref, sems,
):
    q = v_ref.shape[0]
    nocc, halo = pair_ref.shape
    here = table_ref.shape[1] - 2 * halo
    per = v_ref.shape[1] // groups
    blocks_here = here // BB
    first = basis_ref[0] * blocks_here
    copies = [
        pltpu.make_async_copy(v_ref.at[:, pl.ds(g * per, per)], buf_ref.at[g], sems.at[g]) for g in range(groups)
    ]
    columns = chunk_columns(basis_ref[0], *following, carry_ref.shape[1])
    carry = pltpu.make_async_copy(virt_ref.at[pl.ds(0, carry_ref.shape[0]), columns], carry_ref, sems.at[groups])
    for copy in (*copies, carry):
        copy.start()

    acc_ref[...] = jnp.zeros_like(acc_ref)
    odd = basis_ref[0] % 2
    occ_ref[...] = table_ref[...]
    occ_ref[:, pl.ds(pl.multiple_of((1 - odd) * (halo + here), BB), halo)] = pair_ref[...]
    occ_ref[:, pl.ds(pl.multiple_of(odd * (halo + here), BB), halo)] = next_ref[...]

    def picked(k):
        source = lax.rem(map_ref[0, k, 1] - first + NEAR + blocks, blocks)
        rows = occ_ref[:, pl.ds(pl.multiple_of(source * BB, BB), BB)]
        return jnp.where(k < count_ref[0, 0], rows, jnp.zeros_like(rows))

    for g in range(groups):
        copies[g].wait()
        sums = []
        for j in range(0, per, 2):
            k = g * per + j
            if j + 1 < per:
                one, two = picked(k), picked(k + 1)
                none = jnp.zeros_like(one)
                left = jnp.concatenate(
                    [jnp.concatenate([one, none], axis=1), jnp.concatenate([none, two], axis=1)], axis=0
                )
                right = jnp.concatenate([buf_ref[g, :, j], buf_ref[g, :, j + 1]], axis=-1).reshape(q * BB, 2 * BB)
            else:
                left, right = picked(k), buf_ref[g, :, j].reshape(q * BB, BB)
            sums.append(lax.dot_general(left, right, (((1,), (1,)), ((), ())), preferred_element_type=F32))
        for j in range(per):
            rows = sums[j // 2][(j % 2) * nocc : (j % 2 + 1) * nocc]
            target = pl.multiple_of((map_ref[0, g * per + j, 0] - first) * BB, BB)
            for p in range(q):
                acc_ref[p * nocc : (p + 1) * nocc, pl.ds(target, BB)] += rows[:, p * BB : (p + 1) * BB]
    out_ref[...] = acc_ref[...].astype(BF16)
    carry.wait()


def half_rows(basis, pair_map, pair_count, table, pair, after, v_blocks, virt, blocks, width, following):
    q, pairs = v_blocks.shape[:2]
    nocc, halo = pair.shape
    here = table.shape[1] - 2 * halo
    groups = pairs // divisor(pairs, 4)
    return pl.pallas_call(
        functools.partial(half_kernel, groups, blocks, following),
        in_specs=[SMEM, SMEM, SMEM, VMEM, VMEM, VMEM, HBM, HBM],
        out_specs=[VMEM, VMEM],
        scratch_shapes=[
            pltpu.VMEM((groups, q, pairs // groups, BB, BB), BF16),
            pltpu.VMEM((q * nocc, here), F32),
            pltpu.VMEM((nocc, here + 2 * halo), BF16),
            pltpu.SemaphoreType.DMA((groups + 1,)),
        ],
        out_shape=[
            jax.ShapeDtypeStruct((q * nocc, here), BF16),
            jax.ShapeDtypeStruct((carried(virt.shape[0]), width), BF16),
        ],
        compiler_params=pltpu.CompilerParams(vmem_limit_bytes=50 * 2**20),
        cost_estimate=pl.CostEstimate(
            flops=2 * v_blocks.size * nocc, bytes_accessed=2 * v_blocks.size, transcendentals=0
        ),
    )(basis, pair_map, pair_count, table, pair, after, v_blocks, virt)


def carried(depth):
    return min(768, depth // 2)


def cuts_of(depth):
    start = carried(depth)
    return [(at, min(768, depth - at)) for at in range(start, depth, 768)]


def joined(refs):
    return jnp.concatenate([ref[...] for ref in refs], axis=0).astype(F32)


def product_kernel(step, kept, following, parts, adds, basis_ref, virt_ref, first_ref, *refs):
    half_refs, refs = refs[:parts], refs[parts:]
    add_refs = refs[: sum(adds)]
    out_ref, *carry_refs, buf_ref, acc_ref, sems = refs[-5 if following else -4 :]
    width = acc_ref.shape[1]
    columns = chunk_columns(basis_ref[0], step, kept, width)
    cuts = cuts_of(virt_ref.shape[0])
    copies = [
        pltpu.make_async_copy(
            virt_ref.at[pl.ds(start, size), columns], buf_ref.at[pl.ds(start - cuts[0][0], size)], sems.at[i]
        )
        for i, (start, size) in enumerate(cuts)
    ]
    for carry_ref in carry_refs:
        after = chunk_columns(basis_ref[0], *following, width)
        copies.append(
            pltpu.make_async_copy(
                virt_ref.at[pl.ds(0, carry_ref.shape[0]), after], carry_ref, sems.at[len(cuts)]
            )
        )
    for copy in copies:
        copy.start()

    def term(start, block):
        rows = jnp.concatenate([ref[:, start : start + block.shape[0]] for ref in half_refs], axis=0)
        return jnp.dot(rows, block, preferred_element_type=F32)

    total = term(0, first_ref[...])
    at = 0
    for count in adds:
        total += joined(add_refs[at : at + count])
        at += count
    acc_ref[...] = total
    for i, (start, size) in enumerate(cuts):
        copies[i].wait()
        total = acc_ref[...] + term(start, buf_ref[start - cuts[0][0] : start - cuts[0][0] + size])
        if i < len(cuts) - 1:
            acc_ref[...] = total
        else:
            out_ref[...] = total.astype(out_ref.dtype)
    for copy in copies[len(cuts) :]:
        copy.wait()


def product(basis, virt, first, step, kept, following, parts, adds=(), after=(), dtype=BF16):
    rows = sum(part.shape[0] for part in parts)
    depth, width = virt.shape[0], first.shape[1]
    flat = [block for add in adds for block in add]
    shapes = [jax.ShapeDtypeStruct((rows, width), dtype)]
    if following:
        shapes.append(jax.ShapeDtypeStruct(first.shape, BF16))
    return pl.pallas_call(
        functools.partial(product_kernel, step, kept, following, len(parts), tuple(len(add) for add in adds)),
        in_specs=[SMEM, HBM] + [VMEM] * (1 + len(parts) + len(flat)) + [ANY] * len(after),
        out_specs=[VMEM] * len(shapes),
        scratch_shapes=[
            pltpu.VMEM((depth - first.shape[0], width), BF16),
            pltpu.VMEM((rows, width), F32),
            pltpu.SemaphoreType.DMA((len(cuts_of(depth)) + 1,)),
        ],
        out_shape=shapes,
        compiler_params=pltpu.CompilerParams(vmem_limit_bytes=16 * 2**20),
        cost_estimate=pl.CostEstimate(
            flops=2 * rows * depth * width, bytes_accessed=2 * depth * width, transcendentals=0
        ),
    )(basis, virt, first, *parts, *flat, *after)


def finish_kernel(slab, adds, aux_ref, total_ref, *refs):
    add_refs, (out_ref, acc_ref) = refs[: sum(adds)], refs[-2:]
    total = total_ref[...]
    at = 0
    for count in adds:
        total += joined(add_refs[at : at + count])
        at += count
    acc_ref[...] = total
    ordered = [
        acc_ref[pl.ds(pl.multiple_of((aux_ref[0] ^ s) * slab, slab), slab), :]
        for s in range(acc_ref.shape[0] // slab)
    ]
    out_ref[...] = jnp.concatenate(ordered, axis=0).T.astype(BF16)


def finish(aux, total, adds, slab):
    flat = [block for add in adds for block in add]
    return pl.pallas_call(
        functools.partial(finish_kernel, slab, tuple(len(add) for add in adds)),
        in_specs=[SMEM] + [VMEM] * (1 + len(flat)),
        out_specs=VMEM,
        scratch_shapes=[pltpu.VMEM(total.shape, F32)],
        out_shape=jax.ShapeDtypeStruct(total.shape[::-1], BF16),
        compiler_params=pltpu.CompilerParams(vmem_limit_bytes=16 * 2**20),
    )(aux, total, *flat)


def local(v_blocks, pair_map, pair_count, occ_coef, virt_coef):
    peers = lax.axis_size("basis")
    slabs = lax.axis_size("aux")
    aux = lax.axis_index("aux").astype(jnp.int32)
    basis = lax.axis_index("basis").astype(jnp.int32)
    blocks = virt_coef.shape[0] // BB * peers
    halo = NEAR * BB

    even = basis % 2 == 0
    first, last = occ_coef[:, :halo], occ_coef[:, -halo:]
    pair = exchange(jnp.where(even, last, first), "basis", 1)
    ring = [(i, (i + 1 if i % 2 else i - 1) % peers) for i in range(peers)]
    after = lax.ppermute(jnp.where(even, first, last), "basis", ring)
    table = jnp.pad(occ_coef, ((0, 0), (halo, halo)))
    width = virt_coef.shape[1] // peers
    groups = peers // 2
    top, second, *others = range(groups - 1, -1, -1)
    if groups == 4:
        second, others = SECOND, [THIRD, 0]
    sends = [(m, False) for m in (top, second)]
    keeps = [(m, True) for m in (top, second, *others)]
    if groups == 4:
        order = [sends[0], (THIRD, False), *sends, keeps[0], (THIRD, False), *keeps[1:3], (0, False), keeps[3]]
    else:
        order = [sends[0], *sends, *((m, False) for m in others), *keeps]
    number = basis.reshape(1)
    own, first = half_rows(
        number, pair_map, pair_count, table, pair, after, v_blocks, virt_coef, blocks, width, order[0]
    )
    carry = [first]

    def mult(step, kept, parts, adds=(), after=(), dtype=BF16):
        assert order.pop(0) == (step, kept)
        following = order[0] if order else None
        out, *carry[:] = product(number, virt_coef, carry[0], step, kept, following, parts, adds, after, dtype)
        return out

    def send(step, parts, after=()):
        return exchange(mult(step, False, parts, after=after), "basis", 1)

    early = [own, exchange(own, "aux", 1)]
    far = [own]
    bit = slabs // 2
    while bit > 1:
        far += [exchange(rows, "aux", bit) for rows in far]
        bit //= 2
    far = far[1:]
    received = {top: (send(top, early),)}
    if groups == 4:
        received[THIRD] = (send(THIRD, early),)
    *far, _, _ = lax.optimization_barrier((*far, carry[0], received[top][0]))
    late = [block for rows in far for block in (rows, exchange(rows, "aux", 1))]
    every = early + late
    received[top] += (send(top, late),)
    received[second] = (send(second, every, after=received.get(THIRD, ())),)
    if groups == 4:
        sent = mult(3, True, every, (received[3],))
        along = lambda pairs: [(2 * a + s, 2 * b + s) for a, b in pairs for s in (0, 1)]
        inner = lax.ppermute(sent, "basis", along([(1, 2), (2, 1)]))
        relayed = lax.ppermute(sent, "basis", along([(0, 1), (3, 2)]))
        received[THIRD] += (send(THIRD, late),)
        sent = mult(SECOND, True, every, (received[SECOND],))
        third = lax.ppermute(sent, "basis", along([(0, 2), (3, 1), (1, 0), (2, 3)]))
        part = mult(THIRD, True, every, (received[THIRD],), after=(inner, relayed), dtype=F32)
        sent = (part + relayed.astype(F32)).astype(BF16)
        fourth = lax.ppermute(sent, "basis", along([(1, 3), (2, 0), (0, 1), (3, 2)]))
        received[0] = (send(0, every, after=(sent,)),)
        total = mult(0, True, every, dtype=F32)
        total = total + inner.astype(F32) + third.astype(F32)
        total, fourth = lax.optimization_barrier((total, fourth))
        adds = (received[0], (fourth,))
    else:
        for m in others:
            received[m] = (send(m, every),)
        adds = (received[0],)
        for m in (top, second, *others[:-1]):
            sent = mult(m, True, every, (received[m],))
            adds += ((exchange(sent, "basis", 2 * m),),)
        total = mult(0, True, every, dtype=F32)
    return finish(aux.reshape(1), total, adds, own.shape[0])


def solution(mesh):
    in_specs = (
        P("aux", "basis", None, None),
        P("aux", "basis", None),
        P("aux", "basis"),
        P(None, "basis"),
        P("basis", "aux"),
    )
    out_specs = P(("aux", "basis"), None)
    return jax.shard_map(local, mesh=mesh, in_specs=in_specs, out_specs=out_specs, check_vma=False)
```

```python
import functools

import jax
import jax.numpy as jnp
from jax import lax
from jax.experimental import pallas as pl
from jax.experimental.pallas import tpu as pltpu
from jax.sharding import PartitionSpec as P

BB = 128
NEAR = 8
SECOND, THIRD = -1, -2
F32 = jnp.float32
BF16 = jnp.bfloat16
VMEM = pl.BlockSpec(memory_space=pltpu.VMEM)
SMEM = pl.BlockSpec(memory_space=pltpu.SMEM)
HBM = pl.BlockSpec(memory_space=pltpu.HBM)
ANY = pl.BlockSpec(memory_space=pl.ANY)


def exchange(array, axis, bit):
    peers = lax.axis_size(axis)
    return lax.ppermute(array, axis, [(i, i ^ bit) for i in range(peers)])


def divisor(length, most):
    return max(d for d in range(1, most + 1) if length % d == 0)


def chunk_columns(basis, step, kept, width):
    if step in (SECOND, THIRD):
        inside = ((basis >> 1) ^ (basis >> 2)) & 1
        step = 2 - inside if step == SECOND else 1 + inside
    chunk = basis ^ (2 * step + (0 if kept else 1))
    return pl.ds(pl.multiple_of(chunk * width, BB), width)


def half_kernel(
    groups, blocks, following, basis_ref, map_ref, count_ref, table_ref, pair_ref, next_ref, v_ref, virt_ref,
    out_ref, carry_ref, buf_ref, acc_ref, occ_ref, sems,
):
    q = v_ref.shape[0]
    nocc, halo = pair_ref.shape
    here = table_ref.shape[1] - 2 * halo
    per = v_ref.shape[1] // groups
    blocks_here = here // BB
    first = basis_ref[0] * blocks_here
    copies = [
        pltpu.make_async_copy(v_ref.at[:, pl.ds(g * per, per)], buf_ref.at[g], sems.at[g]) for g in range(groups)
    ]
    columns = chunk_columns(basis_ref[0], *following, carry_ref.shape[1])
    carry = pltpu.make_async_copy(virt_ref.at[pl.ds(0, carry_ref.shape[0]), columns], carry_ref, sems.at[groups])
    for copy in (*copies, carry):
        copy.start()

    acc_ref[...] = jnp.zeros_like(acc_ref)
    odd = basis_ref[0] % 2
    occ_ref[...] = table_ref[...]
    occ_ref[:, pl.ds(pl.multiple_of((1 - odd) * (halo + here), BB), halo)] = pair_ref[...]
    occ_ref[:, pl.ds(pl.multiple_of(odd * (halo + here), BB), halo)] = next_ref[...]

    def picked(k):
        source = lax.rem(map_ref[0, k, 1] - first + NEAR + blocks, blocks)
        rows = occ_ref[:, pl.ds(pl.multiple_of(source * BB, BB), BB)]
        return jnp.where(k < count_ref[0, 0], rows, jnp.zeros_like(rows))

    for g in range(groups):
        copies[g].wait()
        sums = []
        for j in range(0, per, 2):
            k = g * per + j
            if j + 1 < per:
                one, two = picked(k), picked(k + 1)
                none = jnp.zeros_like(one)
                left = jnp.concatenate(
                    [jnp.concatenate([one, none], axis=1), jnp.concatenate([none, two], axis=1)], axis=0
                )
                right = jnp.concatenate([buf_ref[g, :, j], buf_ref[g, :, j + 1]], axis=-1).reshape(q * BB, 2 * BB)
            else:
                left, right = picked(k), buf_ref[g, :, j].reshape(q * BB, BB)
            sums.append(lax.dot_general(left, right, (((1,), (1,)), ((), ())), preferred_element_type=F32))
        for j in range(per):
            rows = sums[j // 2][(j % 2) * nocc : (j % 2 + 1) * nocc]
            target = pl.multiple_of((map_ref[0, g * per + j, 0] - first) * BB, BB)
            for p in range(q):
                acc_ref[p * nocc : (p + 1) * nocc, pl.ds(target, BB)] += rows[:, p * BB : (p + 1) * BB]
    out_ref[...] = acc_ref[...].astype(BF16)
    carry.wait()


def half_rows(basis, pair_map, pair_count, table, pair, after, v_blocks, virt, blocks, width, following):
    q, pairs = v_blocks.shape[:2]
    nocc, halo = pair.shape
    here = table.shape[1] - 2 * halo
    groups = pairs // divisor(pairs, 4)
    return pl.pallas_call(
        functools.partial(half_kernel, groups, blocks, following),
        in_specs=[SMEM, SMEM, SMEM, VMEM, VMEM, VMEM, HBM, HBM],
        out_specs=[VMEM, VMEM],
        scratch_shapes=[
            pltpu.VMEM((groups, q, pairs // groups, BB, BB), BF16),
            pltpu.VMEM((q * nocc, here), F32),
            pltpu.VMEM((nocc, here + 2 * halo), BF16),
            pltpu.SemaphoreType.DMA((groups + 1,)),
        ],
        out_shape=[
            jax.ShapeDtypeStruct((q * nocc, here), BF16),
            jax.ShapeDtypeStruct((carried(virt.shape[0]), width), BF16),
        ],
        compiler_params=pltpu.CompilerParams(vmem_limit_bytes=50 * 2**20),
        cost_estimate=pl.CostEstimate(
            flops=2 * v_blocks.size * nocc, bytes_accessed=2 * v_blocks.size, transcendentals=0
        ),
    )(basis, pair_map, pair_count, table, pair, after, v_blocks, virt)


def carried(depth):
    return min(768, depth // 2)


def cuts_of(depth):
    start = carried(depth)
    return [(at, min(768, depth - at)) for at in range(start, depth, 768)]


def joined(refs):
    return jnp.concatenate([ref[...] for ref in refs], axis=0).astype(F32)


def product_kernel(step, kept, following, parts, adds, basis_ref, virt_ref, first_ref, *refs):
    half_refs, refs = refs[:parts], refs[parts:]
    add_refs = refs[: sum(adds)]
    out_ref, *carry_refs, buf_ref, acc_ref, sems = refs[-5 if following else -4 :]
    width = acc_ref.shape[1]
    columns = chunk_columns(basis_ref[0], step, kept, width)
    cuts = cuts_of(virt_ref.shape[0])
    copies = [
        pltpu.make_async_copy(
            virt_ref.at[pl.ds(start, size), columns], buf_ref.at[pl.ds(start - cuts[0][0], size)], sems.at[i]
        )
        for i, (start, size) in enumerate(cuts)
    ]
    for carry_ref in carry_refs:
        after = chunk_columns(basis_ref[0], *following, width)
        copies.append(
            pltpu.make_async_copy(
                virt_ref.at[pl.ds(0, carry_ref.shape[0]), after], carry_ref, sems.at[len(cuts)]
            )
        )
    for copy in copies:
        copy.start()

    def term(start, block):
        rows = jnp.concatenate([ref[:, start : start + block.shape[0]] for ref in half_refs], axis=0)
        return jnp.dot(rows, block, preferred_element_type=F32)

    total = term(0, first_ref[...])
    at = 0
    for count in adds:
        total += joined(add_refs[at : at + count])
        at += count
    acc_ref[...] = total
    for i, (start, size) in enumerate(cuts):
        copies[i].wait()
        total = acc_ref[...] + term(start, buf_ref[start - cuts[0][0] : start - cuts[0][0] + size])
        if i < len(cuts) - 1:
            acc_ref[...] = total
        else:
            out_ref[...] = total.astype(out_ref.dtype)
    for copy in copies[len(cuts) :]:
        copy.wait()


def product(basis, virt, first, step, kept, following, parts, adds=(), after=(), dtype=BF16):
    rows = sum(part.shape[0] for part in parts)
    depth, width = virt.shape[0], first.shape[1]
    flat = [block for add in adds for block in add]
    shapes = [jax.ShapeDtypeStruct((rows, width), dtype)]
    if following:
        shapes.append(jax.ShapeDtypeStruct(first.shape, BF16))
    return pl.pallas_call(
        functools.partial(product_kernel, step, kept, following, len(parts), tuple(len(add) for add in adds)),
        in_specs=[SMEM, HBM] + [VMEM] * (1 + len(parts) + len(flat)) + [ANY] * len(after),
        out_specs=[VMEM] * len(shapes),
        scratch_shapes=[
            pltpu.VMEM((depth - first.shape[0], width), BF16),
            pltpu.VMEM((rows, width), F32),
            pltpu.SemaphoreType.DMA((len(cuts_of(depth)) + 1,)),
        ],
        out_shape=shapes,
        compiler_params=pltpu.CompilerParams(vmem_limit_bytes=16 * 2**20),
        cost_estimate=pl.CostEstimate(
            flops=2 * rows * depth * width, bytes_accessed=2 * depth * width, transcendentals=0
        ),
    )(basis, virt, first, *parts, *flat, *after)


def finish_kernel(slab, adds, aux_ref, total_ref, *refs):
    add_refs, (out_ref, acc_ref) = refs[: sum(adds)], refs[-2:]
    total = total_ref[...]
    at = 0
    for count in adds:
        total += joined(add_refs[at : at + count])
        at += count
    acc_ref[...] = total
    ordered = [
        acc_ref[pl.ds(pl.multiple_of((aux_ref[0] ^ s) * slab, slab), slab), :]
        for s in range(acc_ref.shape[0] // slab)
    ]
    out_ref[...] = jnp.concatenate(ordered, axis=0).T.astype(BF16)


def finish(aux, total, adds, slab):
    flat = [block for add in adds for block in add]
    return pl.pallas_call(
        functools.partial(finish_kernel, slab, tuple(len(add) for add in adds)),
        in_specs=[SMEM] + [VMEM] * (1 + len(flat)),
        out_specs=VMEM,
        scratch_shapes=[pltpu.VMEM(total.shape, F32)],
        out_shape=jax.ShapeDtypeStruct(total.shape[::-1], BF16),
        compiler_params=pltpu.CompilerParams(vmem_limit_bytes=16 * 2**20),
    )(aux, total, *flat)


def local(v_blocks, pair_map, pair_count, occ_coef, virt_coef):
    peers = lax.axis_size("basis")
    slabs = lax.axis_size("aux")
    aux = lax.axis_index("aux").astype(jnp.int32)
    basis = lax.axis_index("basis").astype(jnp.int32)
    blocks = virt_coef.shape[0] // BB * peers
    halo = NEAR * BB

    even = basis % 2 == 0
    first, last = occ_coef[:, :halo], occ_coef[:, -halo:]
    pair = exchange(jnp.where(even, last, first), "basis", 1)
    ring = [(i, (i + 1 if i % 2 else i - 1) % peers) for i in range(peers)]
    after = lax.ppermute(jnp.where(even, first, last), "basis", ring)
    table = jnp.pad(occ_coef, ((0, 0), (halo, halo)))
    width = virt_coef.shape[1] // peers
    groups = peers // 2
    top, second, *others = range(groups - 1, -1, -1)
    if groups == 4:
        second, others = SECOND, [THIRD, 0]
    sends = [(m, False) for m in (top, second)]
    keeps = [(m, True) for m in (top, second, *others)]
    if groups == 4:
        order = [sends[0], (THIRD, False), *sends, keeps[0], (THIRD, False), keeps[1], keeps[3], keeps[2], (0, False)]
    else:
        order = [sends[0], *sends, *((m, False) for m in others), *keeps]
    number = basis.reshape(1)
    own, first = half_rows(
        number, pair_map, pair_count, table, pair, after, v_blocks, virt_coef, blocks, width, order[0]
    )
    carry = [first]

    def mult(step, kept, parts, adds=(), after=(), dtype=BF16):
        assert order.pop(0) == (step, kept)
        following = order[0] if order else None
        out, *carry[:] = product(number, virt_coef, carry[0], step, kept, following, parts, adds, after, dtype)
        return out

    def send(step, parts, after=()):
        return exchange(mult(step, False, parts, after=after), "basis", 1)

    early = [own, exchange(own, "aux", 1)]
    far = [own]
    bit = slabs // 2
    while bit > 1:
        far += [exchange(rows, "aux", bit) for rows in far]
        bit //= 2
    far = far[1:]
    received = {top: (send(top, early),)}
    if groups == 4:
        received[THIRD] = (send(THIRD, early),)
    *far, _, _ = lax.optimization_barrier((*far, carry[0], received[top][0]))
    late = [block for rows in far for block in (rows, exchange(rows, "aux", 1))]
    every = early + late
    received[top] += (send(top, late),)
    received[second] = (send(second, every, after=received.get(THIRD, ())),)
    if groups == 4:
        sent = mult(3, True, every, (received[3],))
        along = lambda pairs: [(2 * a + s, 2 * b + s) for a, b in pairs for s in (0, 1)]
        relayed = lax.ppermute(sent, "basis", along([(0, 1), (3, 2)]))
        inner = lax.ppermute(sent, "basis", along([(1, 2), (2, 1)]))
        received[THIRD] += (send(THIRD, late),)
        sent = mult(SECOND, True, every, (received[SECOND],))
        third = lax.ppermute(sent, "basis", along([(0, 2), (3, 1), (1, 0), (2, 3)]))
        total = mult(0, True, every, dtype=F32)
        part = mult(THIRD, True, every, (received[THIRD],), dtype=F32)
        sent = (part + relayed.astype(F32)).astype(BF16)
        fourth = lax.ppermute(sent, "basis", along([(1, 3), (2, 0), (0, 1), (3, 2)]))
        received[0] = (send(0, every, after=(sent,)),)
        total = total + inner.astype(F32) + third.astype(F32)
        total, fourth = lax.optimization_barrier((total, fourth))
        adds = (received[0], (fourth,))
    else:
        for m in others:
            received[m] = (send(m, every),)
        adds = (received[0],)
        for m in (top, second, *others[:-1]):
            sent = mult(m, True, every, (received[m],))
            adds += ((exchange(sent, "basis", 2 * m),),)
        total = mult(0, True, every, dtype=F32)
    return finish(aux.reshape(1), total, adds, own.shape[0])


def solution(mesh):
    in_specs = (
        P("aux", "basis", None, None),
        P("aux", "basis", None),
        P("aux", "basis"),
        P(None, "basis"),
        P("basis", "aux"),
    )
    out_specs = P(("aux", "basis"), None)
    return jax.shard_map(local, mesh=mesh, in_specs=in_specs, out_specs=out_specs, check_vma=False)
```
